256 devices in a mesh: seq: 64 (over z, y, core), head: 4 (over x).
Axes of the slice: x: 4, y: 4, z: 8, core: 2. Of those that a mesh axis runs over, the one named last changes fastest.
Arguments:
- query_rows: bfloat16 [16384, 4096], P(('seq', 'head')), may hold values from -6 to 6
- key_rows: bfloat16 [16384, 4096], P(('seq', 'head')), may hold values from -6 to 6
- value_rows: bfloat16 [16384, 4096], P(('seq', 'head')), may hold values from -6 to 6
- log_decay: float32 [32, 16384], P('head', 'seq'), may hold values from -1 to 0, as said below
- regularizer: float32 [32], P('head'), may hold values from 0.25 to 2
- norm_gain: float32 [32, 128], P('head'), may hold values from 0.1 to 1.9
- out_weight: bfloat16 [4096, 4096], P('head'), may hold values from -0.09375 to 0.09375
Outputs:
- layer_output: bfloat16 [16384, 4096], P(('seq', 'head'))
The draws below stay inside these ranges and needn't reach their ends.
Inputs may be any that keep to these rules, and one draw needn't show every extreme that they name: `log_decay`: each entry is the logarithm of a forget factor of one head at one token.
All inputs are finite; a program needn't handle non-finite values.
Results may differ from the reference program's by a relative error of at most 0.015.
Values may be sent and summed in bfloat16 or wider, within the bound.
A program may use at most 256 MiB of HBM per device.

```python
import math
import jax
import jax.numpy as jnp
from jax import lax

D = 4096
H = 32
DK = 128
SPAN = 128
ITERS = 4
TOK_DEV = 256
CONTEXT_TOKENS = 16384


def draw_key_rows(key, part):
    key = jax.random.fold_in(key, 11)
    random_splits = jax.random.split(key, 2)
    column_scale = jnp.exp(jax.random.uniform(random_splits[0], (1, H * DK), minval=-2.5, maxval=0.0))
    entries = jnp.clip(jax.random.normal(random_splits[1], (CONTEXT_TOKENS, H * DK)), -4.0, 4.0)
    return (entries * column_scale).astype(jnp.bfloat16)


def draw_value_rows(key, part):
    key = jax.random.fold_in(key, 13)
    random_splits = jax.random.split(key, 2)
    device_blocks = CONTEXT_TOKENS // TOK_DEV
    levels = jnp.exp(jax.random.uniform(random_splits[0], (device_blocks, 1, H, 1), minval=-6.0, maxval=0.4))
    entries = jnp.clip(jax.random.normal(random_splits[1], (device_blocks, TOK_DEV, H, DK)), -4.0, 4.0)
    return (entries * levels).reshape(CONTEXT_TOKENS, H * DK).astype(jnp.bfloat16)


def draw_log_decay(key, part):
    key = jax.random.fold_in(key, 7)
    random_splits = jax.random.split(key, 7)
    slow_share = 0.5
    slow_heads = jax.random.uniform(random_splits[0], (H, 1)) < slow_share
    fast_rate = jnp.exp(jax.random.uniform(random_splits[1], (H, 1), minval=jnp.log(1.0 / 50.0), maxval=jnp.log(1.0 / 20.0)))
    slow_rate = jax.random.uniform(random_splits[2], (H, 1), minval=0.05, maxval=0.5) / CONTEXT_TOKENS
    base_rate = jnp.where(slow_heads, slow_rate, fast_rate)
    device_blocks = CONTEXT_TOKENS // TOK_DEV
    block_factor = jnp.exp(jax.random.uniform(random_splits[3], (H, device_blocks, 1), minval=jnp.log(0.5), maxval=jnp.log(2.0)))
    token_factor = jax.random.uniform(random_splits[4], (H, device_blocks, TOK_DEV), minval=0.5, maxval=1.5)
    decay_speed = (base_rate[:, :, None] * block_factor * token_factor).reshape(H, CONTEXT_TOKENS)
    spike_locations = jax.random.randint(random_splits[5], (2, 1), 0, CONTEXT_TOKENS)
    spike_height = jnp.log(jax.random.uniform(random_splits[6], (2, 1), minval=0.55, maxval=0.8))
    token_places = jnp.arange(CONTEXT_TOKENS)[None, :]
    spike_events = jnp.sum(jnp.where(token_places == spike_locations, spike_height, 0.0), axis=0)
    return (spike_events[None, :] - decay_speed).astype(jnp.float32)


def block_levels(key, shape, cuts, smallest, high):
    def one(axis_at, shards_of):
        heights = jax.random.uniform(jax.random.fold_in(jax.random.fold_in(key, 6), axis_at), (shards_of,), jnp.float32, smallest / len(cuts), high / len(cuts))
        return jnp.repeat(jnp.exp(heights), shape[axis_at] // shards_of).reshape((-1,) + (1,) * (len(shape) - axis_at - 1))

    level = one(*cuts[0])
    for cut in cuts[1:]:
        level = level * one(*cut)
    return level


def noise(stream_key, shape, deviation, reach, cuts=(), dtype=jnp.bfloat16):
    values = jax.random.normal(stream_key, shape, jnp.float32) * deviation
    if len(cuts) > 0:
        values = block_levels(stream_key, shape, cuts, -0.22, 0.18) * values
    return jnp.clip(values, min=-reach, max=reach).astype(dtype)


def setup_inputs(seed: int = 0) -> dict:
    arg_keys = jax.random.split(jax.random.key(seed), 8)
    return {
        "query_rows": noise(arg_keys[0], (CONTEXT_TOKENS, H * DK), 1.0, 6.0, ((0, 256),)),
        "key_rows": draw_key_rows(jax.random.fold_in(arg_keys[7], 71), 0),
        "value_rows": draw_value_rows(jax.random.fold_in(arg_keys[7], 71), 0),
        "log_decay": draw_log_decay(jax.random.fold_in(arg_keys[7], 71), 0),
        "regularizer": jnp.clip(jnp.exp(math.log(2.0) - 2.0794415 * jax.random.uniform(arg_keys[4], (H,), jnp.float32) ** block_levels(arg_keys[4], (H,), ((0, 4),), -0.2, 0.2)), 0.25, 2.0),
        "norm_gain": jnp.clip(1.0 + 0.18 * jax.random.normal(arg_keys[5], (H, DK), jnp.float32), 0.1, 1.9),
        "out_weight": noise(arg_keys[6], (H * DK, D), (H * DK) ** -0.5, 0.09375, ((0, 4),)),
    }


HIGHEST = lax.Precision.HIGHEST
EPSILON = 1e-06

def unit_keys(unscaled):
    head_width = unscaled.shape[-1]
    return unscaled * lax.rsqrt(lax.optimization_barrier(jnp.mean(unscaled * unscaled, axis=-1, keepdims=True)) + EPSILON) * head_width ** (-0.5)

def causal_weights(cumulative):
    length = cumulative.shape[-1]
    spread = cumulative[..., :, None] - cumulative[..., None, :]
    causal_mask = jnp.arange(length)[:, None] >= jnp.arange(length)[None, :]
    return jnp.where(causal_mask, jnp.exp(jnp.minimum(spread, 0.0)), 0.0)

def solve_block(queries, normed_keys, values, cumulative, weights, gram_state, memory, ridge):
    carried = jnp.exp(cumulative)[..., None]
    ridge_term = ridge.reshape(ridge.shape + (1,) * (queries.ndim - 1))

    def operate(vector):
        from_state = carried * jnp.einsum('...cd,...de->...ce', vector, gram_state, precision=HIGHEST)
        correlation = jnp.einsum('...cd,...jd->...cj', vector, normed_keys, precision=HIGHEST) * weights
        return from_state + jnp.einsum('...cj,...jd->...cd', correlation, normed_keys, precision=HIGHEST) + ridge_term * vector
    solution = jnp.zeros_like(queries)
    residual = queries
    direction = queries
    norm_now = lax.optimization_barrier(jnp.sum(residual * residual, axis=-1, keepdims=True))
    for turn_index in range(ITERS):
        mapped = operate(direction)
        step_size = norm_now / lax.optimization_barrier(jnp.sum(direction * mapped, axis=-1, keepdims=True))
        solution = solution + step_size * direction
        if turn_index + 1 < ITERS:
            residual = residual - step_size * mapped
            norm_next = lax.optimization_barrier(jnp.sum(residual * residual, axis=-1, keepdims=True))
            direction = residual + norm_next / norm_now * direction
            norm_now = norm_next
    correlation = jnp.einsum('...cd,...jd->...cj', solution, normed_keys, precision=HIGHEST) * weights
    from_state = carried * jnp.einsum('...cd,...de->...ce', solution, memory, precision=HIGHEST)
    return from_state + jnp.einsum('...cj,...je->...ce', correlation, values, precision=HIGHEST)

def reference(query_rows, key_rows, value_rows, log_decay, regularizer, norm_gain, out_weight):
    blocks = CONTEXT_TOKENS // SPAN

    def arrange(flattened):
        shaped = flattened.astype(jnp.float32).reshape(blocks, SPAN, H, DK)
        return jnp.transpose(shaped, (0, 2, 1, 3))
    queries = arrange(query_rows)
    normed_keys = unit_keys(arrange(key_rows))
    values = arrange(value_rows)
    decays = jnp.transpose(log_decay.reshape(H, blocks, SPAN), (1, 0, 2))

    def advance(state_pair, inputs):
        gram_state, memory = state_pair
        block_query, block_keys, block_values, block_decay = inputs
        cumulative = jnp.cumsum(block_decay, axis=-1)
        weights = causal_weights(cumulative)
        readout = solve_block(block_query, block_keys, block_values, cumulative, weights, gram_state, memory, regularizer)
        scale_back = lax.rsqrt(lax.optimization_barrier(jnp.mean(readout * readout, axis=-1, keepdims=True)) + EPSILON)
        normed = (readout * scale_back * norm_gain[:, None, :]).astype(jnp.bfloat16)
        block_total = cumulative[:, -1:]
        tail_decay = jnp.exp(block_total - cumulative)[..., None]
        factor = jnp.exp(block_total)[..., None]
        gram_next = factor * gram_state + jnp.einsum('hca,hcb->hab', tail_decay * block_keys, block_keys, precision=HIGHEST)
        memory_next = factor * memory + jnp.einsum('hca,hcb->hab', tail_decay * block_keys, block_values, precision=HIGHEST)
        return ((gram_next, memory_next), normed)
    empty_state = jnp.zeros((H, DK, DK), jnp.float32)
    final_pair, normed_all = lax.scan(advance, (empty_state, empty_state), (queries, normed_keys, values, decays))
    readout_rows = jnp.transpose(normed_all, (0, 2, 1, 3)).reshape(CONTEXT_TOKENS, H * DK)
    return jnp.dot(readout_rows, out_weight, preferred_element_type=jnp.float32).astype(jnp.bfloat16)
```

```python
import functools

import jax
import jax.numpy as jnp
from jax import lax
from jax.experimental import pallas as pl
from jax.experimental.pallas import tpu as pltpu
from jax.sharding import PartitionSpec as P

SPAN = 128
ITERS = 4
EPSILON = 1e-06
GROUP = 4
TILE = 512
HIGHEST = lax.Precision.HIGHEST
MESH = pl.DeviceIdType.MESH
F32 = jnp.float32
BF16 = jnp.bfloat16
ROWS_BY_ROWS = (((1,), (1,)), ((), ()))
COLS_BY_COLS = (((0,), (0,)), ((), ()))


def kernel(
    planes, inner, ring,
    q_hbm, k_hbm, v_hbm, ld_ref, reg_ref, gain_ref, w_hbm, out_ref,
    qb, kb, vb, wv, weights, carried, tails, totals, knorm, first,
    dec, dec_plane, dec_ztot, dec_z,
    state_out, state_plane, ptot, z_in, z_out, z_state, back_out, start,
    solved, readout, partial32, partial, relay_a, relay_b, n1_a, n1_b, n2_a, n2_b, comb_a, comb_b,
    local_sem, x_send, x_recv, dp_send, dp_recv, dz_send, dz_recv,
    p_send, p_recv, z_send, z_recv, zb_send, zb_recv, b_send, b_recv, r_send, r_recv,
):
    s = lax.axis_index("seq")
    x = lax.axis_index("head")
    z = lax.div(s, inner)
    me = lax.rem(s, inner)
    rows = q_hbm.shape[0]
    width = kb.shape[1]
    heads = ld_ref.shape[0]
    half = w_hbm.shape[1] // 2
    pending = []

    def to_plane(peer):
        return (z * inner + peer, x)

    def to_z(peer):
        return (peer * inner + me, x)

    def to_x(peer):
        return (s, peer)

    def remote(src, dst, send, recv, device):
        return pltpu.make_async_remote_copy(
            src_ref=src, dst_ref=dst, send_sem=send, recv_sem=recv,
            device_id=device, device_id_type=MESH,
        )

    def exchange(count, here, device, make, send, recv):
        def each(fn):
            def step(o, carry):
                fn(o)
                return carry
            lax.fori_loop(1, count, step, 0)

        def go(o):
            peer = lax.rem(here + o, count)
            src, dst = make(peer, here)
            remote(src, dst, send(o - 1), recv(o - 1), device(peer)).start()

        def got(o):
            peer = lax.rem(here + count - o, count)
            src, dst = make(here, peer)
            remote(src, dst, send(o - 1), recv(o - 1), device(peer)).wait_recv()

        def sent(o):
            peer = lax.rem(here + o, count)
            src, dst = make(peer, here)
            remote(src, dst, send(o - 1), recv(o - 1), device(peer)).wait_send()

        each(go)
        pending.append(lambda: each(sent))
        return lambda: each(got)

    barrier = pltpu.get_barrier_semaphore()
    for count, here, device in ((ring, x, to_x), (inner, me, to_plane), (planes, z, to_z)):
        def greet(o, carry, count=count, here=here, device=device):
            pl.semaphore_signal(
                barrier, inc=1, device_id=device(lax.rem(here + o, count)), device_id_type=MESH
            )
            return carry
        lax.fori_loop(1, count, greet, 0)
    pl.semaphore_wait(barrier, ring + inner + planes - 3)

    x_done = []
    for i, (src_hbm, dst_buf) in enumerate(((k_hbm, kb), (v_hbm, vb), (q_hbm, qb))):
        mine = pltpu.make_async_copy(
            src_hbm.at[:, pl.ds(pl.multiple_of(x * width, width), width)],
            dst_buf.at[pl.ds(pl.multiple_of(x * rows, rows), rows), :],
            local_sem.at[i],
        )
        mine.start()

        def make(to, frm, src_hbm=src_hbm, dst_buf=dst_buf):
            return (
                src_hbm.at[:, pl.ds(pl.multiple_of(to * width, width), width)],
                dst_buf.at[pl.ds(pl.multiple_of(frm * rows, rows), rows), :],
            )

        got = exchange(
            ring, x, to_x, make,
            lambda o, i=i: x_send.at[i, o], lambda o, i=i: x_recv.at[i, o],
        )
        x_done.append((mine, got))
    w_copy = pltpu.make_async_copy(w_hbm, wv, local_sem.at[3])
    w_copy.start()

    row_id = lax.broadcasted_iota(jnp.int32, (SPAN, SPAN), 0)
    col_id = lax.broadcasted_iota(jnp.int32, (SPAN, SPAN), 1)
    causal = row_id >= col_id
    lower = jnp.where(causal, 1.0, 0.0).astype(F32)

    def head_row(table, h):
        place = lax.broadcasted_iota(jnp.int32, table.shape, 0)
        return jnp.sum(jnp.where(place == h, table, 0.0), axis=0, keepdims=True)

    def prepare(h, carry):
        total = None
        for n in range(2):
            spread_row = jnp.broadcast_to(
                head_row(ld_ref[:, n * SPAN:(n + 1) * SPAN], h), (SPAN, SPAN)
            )
            cum = lax.dot_general(
                lower, spread_row, ROWS_BY_ROWS, precision=HIGHEST, preferred_element_type=F32
            )
            cum_row = lax.dot_general(
                spread_row, lower, ROWS_BY_ROWS, precision=HIGHEST, preferred_element_type=F32
            )
            weights[n, h] = jnp.where(causal, jnp.exp(jnp.minimum(cum - cum_row, 0.0)), 0.0)
            carried[n, h] = jnp.exp(cum)
            last = cum[SPAN - 1:SPAN, :]
            tails[n, h] = jnp.exp(last - cum)
            totals[n, h] = jnp.broadcast_to(last, (8, SPAN))
            total = last if total is None else total + last
        dec[h] = jnp.broadcast_to(total, (8, SPAN))
        return carry

    lax.fori_loop(0, heads, prepare, 0)

    got_dec = exchange(
        inner, me, to_plane, lambda to, frm: (dec.at[to], dec_plane.at[frm]),
        lambda o: dp_send.at[o], lambda o: dp_recv.at[o],
    )
    dec_plane[me] = dec[me]
    got_dec()

    dec_ztot[...] = lax.fori_loop(
        0, inner, lambda i, acc: acc + dec_plane[i], jnp.zeros((8, SPAN), F32)
    )
    got_decz = exchange(
        planes, z, to_z, lambda to, frm: (dec_ztot, dec_z.at[frm]),
        lambda o: dz_send.at[o], lambda o: dz_recv.at[o],
    )
    dec_z[z] = dec_ztot[...]
    got_decz()

    def wait_x(i):
        mine, got = x_done[i]
        mine.wait()
        got()

    def head_cols(h):
        return pl.ds(pl.multiple_of(h * SPAN, SPAN), SPAN)

    def local_state(t):
        def one(h, carry):
            terms = []
            for n in range(2):
                if t == 0:
                    key = kb[n * SPAN:(n + 1) * SPAN, head_cols(h)].astype(F32)
                    square = jnp.mean(key * key, axis=-1, keepdims=True)
                    normed = key * (lax.rsqrt(square + EPSILON) * SPAN ** -0.5)
                    right = normed.astype(BF16)
                    knorm[n, h] = right
                    tails[n, h] = tails[n, h] * normed
                else:
                    right = vb[n * SPAN:(n + 1) * SPAN, head_cols(h)]
                terms.append(
                    lax.dot_general(
                        tails[n, h].astype(BF16), right, COLS_BY_COLS, preferred_element_type=F32
                    )
                )
            first[t, h] = terms[0]
            factor = jnp.exp(totals[1, h][0:1, :])
            state_out[t, h] = (factor * terms[0] + terms[1]).astype(BF16)
            return carry

        lax.fori_loop(0, heads, one, 0)

    def send_plane(t):
        got = exchange(
            inner, me, to_plane,
            lambda to, frm: (state_out.at[t, to], state_plane.at[t, frm]),
            lambda o: p_send.at[t, o], lambda o: p_recv.at[t, o],
        )
        state_plane[t, me] = state_out[t, me]
        return got

    def plane_total(t):
        def step(i, acc):
            return jnp.exp(dec_plane[i][0:1, :]) * acc + state_plane[t, i].astype(F32)

        ptot[t] = lax.fori_loop(0, inner, step, jnp.zeros((SPAN, SPAN), F32)).astype(BF16)

    piece = SPAN // planes

    def piece_rows(i):
        return pl.ds(pl.multiple_of(i * piece, piece), piece)

    def send_z(t):
        got = exchange(
            planes, z, to_z,
            lambda to, frm: (ptot.at[t, piece_rows(to), :], z_in.at[t, frm]),
            lambda o: z_send.at[t, o], lambda o: z_recv.at[t, o],
        )
        z_in[t, z] = ptot[t, piece_rows(z), :]
        return got

    def z_prefix(t):
        def step(i, acc):
            z_out[t, i] = acc.astype(BF16)
            return jnp.exp(dec_z[i][0:1, :]) * acc + z_in[t, i].astype(F32)

        lax.fori_loop(0, planes, step, jnp.zeros((piece, SPAN), F32))

    def send_z_back(t):
        got = exchange(
            planes, z, to_z,
            lambda to, frm: (z_out.at[t, to], z_state.at[t, piece_rows(frm), :]),
            lambda o: zb_send.at[t, o], lambda o: zb_recv.at[t, o],
        )
        z_state[t, piece_rows(z), :] = z_out[t, z]
        return got

    def plane_prefix(t):
        def step(i, acc):
            back_out[t, i] = acc.astype(BF16)
            return jnp.exp(dec_plane[i][0:1, :]) * acc + state_plane[t, i].astype(F32)

        lax.fori_loop(0, inner, step, z_state[t].astype(F32))

    def send_back(t):
        got = exchange(
            inner, me, to_plane,
            lambda to, frm: (back_out.at[t, to], start.at[t, frm]),
            lambda o: b_send.at[t, o], lambda o: b_recv.at[t, o],
        )
        start[t, me] = back_out[t, me]
        return got

    wait_x(0)
    local_state(0)
    got_p0 = send_plane(0)
    got_p0()
    plane_total(0)
    got_z0 = send_z(0)
    wait_x(1)
    local_state(1)
    got_p1 = send_plane(1)
    got_z0()
    z_prefix(0)
    got_zb0 = send_z_back(0)
    got_p1()
    plane_total(1)
    got_z1 = send_z(1)
    got_zb0()
    plane_prefix(0)
    got_b0 = send_back(0)
    got_z1()
    z_prefix(1)
    got_zb1 = send_z_back(1)
    got_zb1()
    plane_prefix(1)
    got_b1 = send_back(1)
    got_b0()
    wait_x(2)
    def block_rows(n):
        return pl.ds(pl.multiple_of(n * SPAN, SPAN), SPAN)

    def start_state(t, n, h):
        later = jnp.where(n == 1, 1.0, 0.0).astype(F32)
        factor = jnp.where(n == 1, jnp.exp(totals[0, h][0:1, :]), 1.0)
        return (factor * start[t, h].astype(F32) + later * first[t, h]).astype(BF16)

    def row_sum(a):
        return jnp.sum(a, axis=-1, keepdims=True)

    def solve(n):
        def solve_group(g, carry):
            hs = [g * GROUP + i for i in range(GROUP)]
            each = range(GROUP)
            keys = [knorm[n, h] for h in hs]
            mixed = [jnp.concatenate([start_state(0, n, h), knorm[n, h]], axis=0) for h in hs]
            direction = [qb[block_rows(n), head_cols(h)].astype(F32) for h in hs]
            residual = list(direction)
            answer = [None] * GROUP
            norm_now = [row_sum(r * r) for r in residual]
            for turn in range(ITERS):
                corr = [
                    lax.dot_general(
                        direction[i].astype(BF16), keys[i], ROWS_BY_ROWS,
                        preferred_element_type=F32,
                    )
                    for i in each
                ]
                left = [
                    jnp.concatenate(
                        [
                            (carried[n, hs[i]] * direction[i]).astype(BF16),
                            (corr[i] * weights[n, hs[i]]).astype(BF16),
                        ],
                        axis=1,
                    )
                    for i in each
                ]
                mapped = [
                    jnp.dot(left[i], mixed[i], preferred_element_type=F32)
                    + reg_ref[hs[i]] * direction[i]
                    for i in each
                ]
                step_size = [norm_now[i] / row_sum(direction[i] * mapped[i]) for i in each]
                answer = [
                    step_size[i] * direction[i]
                    if turn == 0
                    else answer[i] + step_size[i] * direction[i]
                    for i in each
                ]
                if turn + 1 < ITERS:
                    residual = [residual[i] - step_size[i] * mapped[i] for i in each]
                    norm_next = [row_sum(r * r) for r in residual]
                    direction = [
                        residual[i] + norm_next[i] / norm_now[i] * direction[i] for i in each
                    ]
                    norm_now = norm_next
            for i in each:
                solved[g * GROUP + i] = answer[i]
            return carry

        lax.fori_loop(0, heads // GROUP, solve_group, 0)

    def read(n):
        def read_group(g, carry):
            hs = [g * GROUP + i for i in range(GROUP)]
            for h in hs:
                answer = solved[h]
                corr = lax.dot_general(
                    answer.astype(BF16), knorm[n, h], ROWS_BY_ROWS, preferred_element_type=F32
                )
                left = jnp.concatenate(
                    [
                        (carried[n, h] * answer).astype(BF16),
                        (corr * weights[n, h]).astype(BF16),
                    ],
                    axis=1,
                )
                mixed = jnp.concatenate(
                    [start_state(1, n, h), vb[block_rows(n), head_cols(h)]], axis=0
                )
                raw = jnp.dot(left, mixed, preferred_element_type=F32)
                scale = lax.rsqrt(jnp.mean(raw * raw, axis=-1, keepdims=True) + EPSILON)
                readout[:, head_cols(h)] = (raw * scale * head_row(gain_ref[...], h)).astype(BF16)
            return carry

        lax.fori_loop(0, heads // GROUP, read_group, 0)

    def project(lo, hi):
        def tile(c, carry):
            cols = pl.ds(pl.multiple_of(c * TILE, TILE), TILE)
            partial32[:, cols] = jnp.dot(
                readout[...], wv[:, cols], preferred_element_type=F32
            )
            return carry

        lax.fori_loop(lo // TILE, hi // TILE, tile, 0)

    far, near_1, near_2 = x ^ 2, x ^ 3, x ^ 1
    r_done = {}

    def slot(chunk):
        return pl.ds(pl.multiple_of(lax.rem(chunk, 2) * rows, rows), rows)

    def columns(side):
        return slice(0, half) if side == 0 else slice(half, 2 * half)

    def send_result(i, src, dst, peer):
        copy = remote(src, dst, r_send.at[i], r_recv.at[i], to_x(peer))
        copy.start()
        pending.append(copy.wait_send)
        r_done[i] = copy.wait_recv

    n = 1 - lax.div(x, 2)
    solve(n)
    got_b1()
    read(n)
    w_copy.wait()
    for side in range(2):
        project(side * half, (side + 1) * half)
        partial[0, :, columns(side)] = partial32[:, columns(side)].astype(BF16)
        src = partial.at[0, slot(far), columns(side)]
        if side == 0:
            send_result(0, src, relay_a, near_1)
            send_result(1, partial.at[0, slot(near_1), columns(0)], n1_a, near_1)
        else:
            send_result(2, src, relay_b, near_2)

    n = lax.div(x, 2)
    solve(n)
    read(n)
    r_done.pop(2)()
    comb_b[...] = (
        partial[0, slot(near_1), columns(1)].astype(F32) + relay_b[...].astype(F32)
    ).astype(BF16)
    send_result(3, comb_b, n1_b, near_1)
    project(half, 2 * half)
    partial[1, :, columns(1)] = partial32[:, columns(1)].astype(BF16)
    send_result(4, partial.at[1, slot(near_2), columns(1)], n2_b, near_2)
    project(0, half)
    r_done.pop(0)()
    comb_a[...] = (partial32[slot(near_2), columns(0)] + relay_a[...].astype(F32)).astype(BF16)
    send_result(5, comb_a, n2_a, near_2)
    for i in (1, 3, 4, 5):
        r_done.pop(i)()
    out_ref[:, columns(0)] = (
        partial32[slot(x), columns(0)] + n1_a[...].astype(F32) + n2_a[...].astype(F32)
    ).astype(BF16)
    out_ref[:, columns(1)] = (
        partial32[slot(x), columns(1)] + n1_b[...].astype(F32) + n2_b[...].astype(F32)
    ).astype(BF16)
    for fn in pending:
        fn()


def body(planes, inner, query_rows, key_rows, value_rows, log_decay, regularizer, norm_gain, out_weight):
    ring = lax.axis_size("head")
    rows, model = query_rows.shape
    heads = regularizer.shape[0]
    width = heads * SPAN
    tokens = rows * ring
    half = model // 2
    vm = pltpu.VMEM
    dma = pltpu.SemaphoreType.DMA
    piece = SPAN // planes
    scratch = [
        vm((tokens, width), BF16),
        vm((tokens, width), BF16),
        vm((tokens, width), BF16),
        vm((width, model), BF16),
        vm((2, heads, SPAN, SPAN), F32),
        vm((2, heads, SPAN, SPAN), F32),
        vm((2, heads, SPAN, SPAN), F32),
        vm((2, heads, 8, SPAN), F32),
        vm((2, heads, SPAN, SPAN), BF16),
        vm((2, heads, SPAN, SPAN), F32),
        vm((heads, 8, SPAN), F32),
        vm((inner, 8, SPAN), F32),
        vm((8, SPAN), F32),
        vm((planes, 8, SPAN), F32),
        vm((2, heads, SPAN, SPAN), BF16),
        vm((2, inner, SPAN, SPAN), BF16),
        vm((2, SPAN, SPAN), BF16),
        vm((2, planes, piece, SPAN), BF16),
        vm((2, planes, piece, SPAN), BF16),
        vm((2, SPAN, SPAN), BF16),
        vm((2, inner, SPAN, SPAN), BF16),
        vm((2, heads, SPAN, SPAN), BF16),
        vm((heads, SPAN, SPAN), F32),
        vm((SPAN, width), BF16),
        vm((SPAN, model), F32),
        vm((2, SPAN, model), BF16),
    ]
    scratch += [vm((rows, half), BF16)] * 8
    scratch += [dma((4,)), dma((3, ring - 1)), dma((3, ring - 1))]
    scratch += [dma((inner - 1,))] * 2 + [dma((planes - 1,))] * 2
    scratch += [dma((2, inner - 1))] * 2 + [dma((2, planes - 1))] * 4 + [dma((2, inner - 1))] * 2
    scratch += [dma((6,))] * 2
    anywhere = pl.BlockSpec(memory_space=pl.ANY)
    local = pl.BlockSpec(memory_space=pltpu.VMEM)
    return pl.pallas_call(
        functools.partial(kernel, planes, inner, ring),
        out_shape=jax.ShapeDtypeStruct((rows, model), BF16),
        in_specs=[
            anywhere, anywhere, anywhere, local,
            pl.BlockSpec(memory_space=pltpu.SMEM), local, anywhere,
        ],
        out_specs=local,
        scratch_shapes=scratch,
        compiler_params=pltpu.CompilerParams(
            collective_id=0, has_side_effects=True, vmem_limit_bytes=48 * 1024 * 1024
        ),
    )(query_rows, key_rows, value_rows, log_decay, regularizer, norm_gain, out_weight)


def solution(mesh):
    placed = (
        P(("seq", "head"), None),
        P(("seq", "head"), None),
        P(("seq", "head"), None),
        P("head", "seq"),
        P("head"),
        P("head", None),
        P("head", None),
    )
    inner = 8
    planes = mesh.shape["seq"] // inner
    return jax.shard_map(
        functools.partial(body, planes, inner), mesh=mesh, in_specs=placed,
        out_specs=P(("seq", "head"), None), check_vma=False,
    )
```

```python
import functools

import jax
import jax.numpy as jnp
from jax import lax
from jax.experimental import pallas as pl
from jax.experimental.pallas import tpu as pltpu
from jax.sharding import PartitionSpec as P

SPAN = 128
ITERS = 4
EPSILON = 1e-06
TILE = 512
BATCH = 2
MESH = pl.DeviceIdType.MESH
HIGHEST = lax.Precision.HIGHEST
F32 = jnp.float32
BF16 = jnp.bfloat16
ROWS_BY_ROWS = (((1,), (1,)), ((), ()))
COLS_BY_COLS = (((0,), (0,)), ((), ()))


def kernel(
    planes, inner, ring,
    q_hbm, k_hbm, v_hbm, ld_hbm, reg_hbm, gain_hbm, w_hbm, out_ref,
    ld_plane, reg_ref, gain_ref, qb, kb, vb, wv, weights, carried, tails, leave, enter, dec_total,
    knorm, klow, tailed, terms, before, z_to, z_in, z_out, z_back, z_state,
    solved, sending, readout, own, partial,
    relay_a, relay_b, n1_a, n1_b, n2_a, n2_b,
    local_sem, ld_send, ld_recv, g_send, g_recv,
    z_send, z_recv, zb_send, zb_recv, b_send, b_recv, r_send, r_recv,
):
    s = lax.axis_index("seq")
    x = lax.axis_index("head")
    z = lax.div(s, inner)
    me = lax.rem(s, inner)
    rows = q_hbm.shape[0]
    blocks = knorm.shape[0]
    per_device = blocks // inner
    half = w_hbm.shape[1] // 2
    pending = []

    def loop(lo, hi, fn):
        def step(i, carry):
            fn(i)
            return carry
        lax.fori_loop(lo, hi, step, 0)

    def shift_plane(o, sign):
        return lax.rem(me + inner + sign * o, inner)

    def shift_z(o, sign):
        return lax.rem(z + planes + sign * o, planes)

    def shift_group(o, sign):
        over = lax.div(o, ring)
        along = lax.rem(o, ring)
        return (
            lax.rem(me + inner + sign * over, inner), lax.rem(x + ring + sign * along, ring)
        )

    def shift_far(mask):
        return lambda o, sign: (lax.rem(me + inner + sign * o, inner), x ^ mask)

    def in_group(peer):
        return (z * inner + peer[0], peer[1])

    plane = (1, inner, shift_plane, lambda peer: (z * inner + peer, x))
    column = (1, planes, shift_z, lambda peer: (peer * inner + me, x))
    group = (1, inner * ring, shift_group, in_group)
    kinds = [(0 if mask else 1, inner, shift_far(mask), in_group) for mask in (2, 3, 1, 0)]

    def remote(src, dst, send, recv, device):
        return pltpu.make_async_remote_copy(
            src_ref=src, dst_ref=dst, send_sem=send, recv_sem=recv,
            device_id=device, device_id_type=MESH,
        )

    def exchange(partners, make_pair, send, recv, here, later=False):
        first, count, shift, device = partners

        def copy(o, sign):
            peer = shift(o, sign)
            src, dst = make_pair(peer, here) if sign == 1 else make_pair(here, peer)
            return remote(src, dst, send(o), recv(o), device(peer))

        pending.append(lambda: loop(first, count, lambda o: copy(o, 1).wait_send()))
        if later:
            return (lambda o: copy(o, 1).start()), (lambda o: copy(o, -1).wait_recv())
        loop(first, count, lambda o: copy(o, 1).start())
        return lambda o: copy(o, -1).wait_recv()

    def all_of(partners, got):
        loop(partners[0], partners[1], got)

    small = [
        pltpu.make_async_copy(src, dst, local_sem.at[i])
        for i, (src, dst) in enumerate(
            ((ld_hbm, ld_plane.at[me]), (reg_hbm, reg_ref), (gain_hbm, gain_ref))
        )
    ]
    for copy in small:
        copy.start()

    barrier = pltpu.get_barrier_semaphore()
    for _, count, shift, device in (group, column):
        loop(
            1, count,
            lambda o, shift=shift, device=device: pl.semaphore_signal(
                barrier, inc=1, device_id=device(shift(o, 1)), device_id_type=MESH
            ),
        )
    pl.semaphore_wait(barrier, inner * ring - 1 + planes - 1)

    got_ld = exchange(
        plane, lambda to, frm: (ld_hbm, ld_plane.at[frm]),
        lambda o: ld_send.at[o], lambda o: ld_recv.at[o], me,
    )

    def slot(place):
        return pl.ds(pl.multiple_of((place[0] * ring + place[1]) * rows, rows), rows)

    def head_cols(place):
        return pl.ds(pl.multiple_of((place[1] * inner + place[0]) * SPAN, SPAN), SPAN)

    got_group = []
    for i, (src_hbm, dst_buf) in enumerate(((k_hbm, kb), (v_hbm, vb), (q_hbm, qb))):
        def make(to, frm, src_hbm=src_hbm, dst_buf=dst_buf):
            return src_hbm.at[:, head_cols(to)], dst_buf.at[slot(frm), :]

        mine = pltpu.make_async_copy(*make((me, x), (me, x)), local_sem.at[3 + i])
        mine.start()
        parts = [group] if i < 2 else kinds
        moves = [
            exchange(
                part, make,
                lambda o, i=i, at=n * inner: g_send.at[i, at + o],
                lambda o, i=i, at=n * inner: g_recv.at[i, at + o],
                (me, x), later=True,
            )
            for n, part in enumerate(parts)
        ]
        got_group.append((mine, moves))

    def go_group(i, n=0):
        part = group if i < 2 else kinds[n]
        loop(part[0], part[1], got_group[i][1][n][0])

    go_group(0)
    go_group(1)
    w_copy = pltpu.make_async_copy(w_hbm, wv, local_sem.at[6])

    def pick_row(table, i):
        place = lax.broadcasted_iota(jnp.int32, table.shape, 0)
        return jnp.sum(jnp.where(place == i, table, 0.0), axis=0, keepdims=True)

    row_id = lax.broadcasted_iota(jnp.int32, (SPAN, SPAN), 0)
    col_id = lax.broadcasted_iota(jnp.int32, (SPAN, SPAN), 1)
    causal = row_id >= col_id
    for copy in small:
        copy.wait()
    all_of(plane, got_ld)

    def down(row):
        return jnp.transpose(jnp.broadcast_to(row, (SPAN, SPAN)))

    sums = lax.dot_general(
        jnp.concatenate(
            [
                pick_row(ld_plane[b // per_device][:, (b % per_device) * SPAN:(b % per_device + 1) * SPAN], me)
                for b in range(blocks)
            ],
            axis=0,
        ),
        jnp.where(causal, 1.0, 0.0).astype(F32),
        ROWS_BY_ROWS, precision=HIGHEST, preferred_element_type=F32,
    )
    total = jnp.zeros((8, SPAN), F32)
    for b in range(blocks):
        row = sums[b:b + 1, :]
        last = jnp.broadcast_to(row[:, SPAN - 1:SPAN], (8, SPAN))
        enter[b] = jnp.exp(total)
        total = total + last
        cum = down(row)
        tails[b] = jnp.exp(last[0:1, :] - cum)
        weights[b] = jnp.where(causal, jnp.exp(jnp.minimum(cum - row, 0.0)), 0.0)
        carried[b] = jnp.exp(cum)
        leave[b] = jnp.exp(last)
    dec_total[...] = total

    def split(value):
        high = value.astype(BF16)
        return high, (value - high.astype(F32)).astype(BF16)

    def block_rows(b):
        return pl.ds(pl.multiple_of(b * SPAN, SPAN), SPAN)

    def plane_states(t):
        mine, ((_, got),) = got_group[t]

        def states(over):
            source = lax.rem(me + inner - over, inner)
            for n in range(per_device):
                b = source * per_device + n
                if t == 0:
                    key = kb[block_rows(b), :].astype(F32)
                    square = jnp.mean(key * key, axis=-1, keepdims=True)
                    normed = key * (lax.rsqrt(square + EPSILON) * SPAN ** -0.5)
                    right, right_low = split(normed)
                    knorm[b] = right
                    klow[b] = right_low
                    left, left_low = split(tails[b] * normed)
                    tailed[b] = left
                    left = jnp.concatenate([left, left_low, left], axis=0)
                    right = jnp.concatenate([right, right, right_low], axis=0)
                else:
                    right = vb[block_rows(b), :]
                    left = tailed[b]
                terms[b] = lax.dot_general(
                    left, right, COLS_BY_COLS, preferred_element_type=F32
                )

        def batch(i):
            if isinstance(i, int):
                mine.wait()
                loop(1, BATCH * ring, got)
            else:
                loop(i * BATCH * ring, (i + 1) * BATCH * ring, got)
            for n in range(BATCH):
                states(i * BATCH + n)

        batch(0)
        loop(1, inner // BATCH, batch)
        plane_total = jnp.zeros((SPAN, SPAN), F32)
        for b in range(blocks):
            before[t, b] = plane_total
            plane_total = leave[b][0:1, :] * plane_total + terms[b]
        for i in range(planes):
            rows_of = plane_total[i * piece:(i + 1) * piece, :]
            if t == 0:
                z_to[i, 0:piece, :], z_to[i, piece:2 * piece, :] = split(rows_of)
            else:
                z_to[i, 2 * piece:3 * piece, :] = rows_of.astype(BF16)

    piece = SPAN // planes

    def send_z():
        rest = dec_total[0:1, :]
        terms_of = []
        for _ in range(3):
            term = rest.astype(BF16)
            terms_of.append(jnp.broadcast_to(term.astype(F32), (8, SPAN)))
            rest = rest - term.astype(F32)
        place = lax.broadcasted_iota(jnp.int32, (piece, SPAN), 0)
        packed = jnp.zeros((piece, SPAN), F32)
        for i, term in enumerate(terms_of):
            packed = jnp.where(place == i, term[0:1, :], packed)
        packed = packed.astype(BF16)
        for i in range(planes):
            z_to[i, 3 * piece:4 * piece, :] = packed
        got = exchange(
            column, lambda to, frm: (z_to.at[to], z_in.at[frm]),
            lambda o: z_send.at[o], lambda o: z_recv.at[o], z,
        )
        z_in[z] = z_to[z]
        return got

    def z_prefix():
        gram = jnp.zeros((piece, SPAN), F32)
        memory = gram
        for i in range(planes):
            z_out[i, 0:piece, :], z_out[i, piece:2 * piece, :] = split(gram)
            z_out[i, 2 * piece:3 * piece, :] = memory.astype(BF16)
            if i + 1 < planes:
                arrived = z_in[i].astype(F32)
                tail = arrived[3 * piece:4 * piece, :]
                decay = jnp.exp(tail[0:1, :] + tail[1:2, :] + tail[2:3, :])
                gram = decay * gram + (arrived[0:piece, :] + arrived[piece:2 * piece, :])
                memory = decay * memory + arrived[2 * piece:3 * piece, :]

    def send_z_back():
        got = exchange(
            column, lambda to, frm: (z_out.at[to], z_back.at[frm]),
            lambda o: zb_send.at[o], lambda o: zb_recv.at[o], z,
        )
        z_back[z] = z_out[z]
        return got

    def collect():
        for i in range(planes):
            arrived = z_back[i].astype(F32)
            here = slice(i * piece, (i + 1) * piece)
            z_state[0, here, :] = arrived[0:piece, :] + arrived[piece:2 * piece, :]
            z_state[1, here, :] = arrived[2 * piece:3 * piece, :]

    def wait_queries(kind):
        mine, moves = got_group[2]
        if kind == 3:
            mine.wait()
        all_of(kinds[kind], moves[kind][1])

    plane_states(0)
    plane_states(1)
    got_z = send_z()
    for kind in range(4):
        go_group(2, kind)
    all_of(column, got_z)
    z_prefix()
    got_zb = send_z_back()
    w_copy.start()
    wait_queries(0)
    all_of(column, got_zb)
    collect()

    def start_state(t, b):
        return enter[b][0:1, :] * z_state[t] + before[t, b]

    def row_sum(a):
        return jnp.sum(a, axis=-1, keepdims=True)

    chunks = [x ^ mask for mask in (2, 3, 1, 0)]

    def member(i):
        return lax.rem(me + 1 + i, inner)

    def block_of(kind, i):
        return member(i) * per_device + lax.div(chunks[kind], ring // per_device)

    def token_rows(kind):
        return pl.ds(
            pl.multiple_of(lax.rem(chunks[kind], ring // per_device) * rows, rows), rows
        )

    def correlate(vector, b):
        high, low = split(vector)
        key = knorm[b]
        return lax.dot_general(
            jnp.concatenate([high, low], axis=1), jnp.concatenate([key, key], axis=1),
            ROWS_BY_ROWS, preferred_element_type=F32,
        ) + lax.dot_general(high, klow[b], ROWS_BY_ROWS, preferred_element_type=F32)

    def solve(kind):
        each = range(inner)
        bs = [block_of(kind, i) for i in each]
        here = token_rows(kind)
        ridge = reg_ref[me]
        states = [split(start_state(0, b)) for b in bs]
        mixed = [
            jnp.concatenate([states[i][0], knorm[bs[i]], states[i][0], knorm[bs[i]]], axis=0)
            for i in each
        ]
        mixed_low = [jnp.concatenate([states[i][1], klow[bs[i]]], axis=0) for i in each]
        direction = [qb[slot((member(i), chunks[kind])), :].astype(F32) for i in each]
        residual = list(direction)
        answer = [None] * inner
        norm_now = [row_sum(r * r) for r in residual]
        for turn in range(ITERS):
            corr = [correlate(direction[i], bs[i]) for i in each]
            from_state = [split(carried[bs[i], here, :] * direction[i]) for i in each]
            from_block = [split(corr[i] * weights[bs[i], here, :]) for i in each]
            high = [
                jnp.concatenate([from_state[i][0], from_block[i][0]], axis=1) for i in each
            ]
            both = [
                jnp.concatenate([high[i], from_state[i][1], from_block[i][1]], axis=1)
                for i in each
            ]
            mapped = [
                jnp.dot(both[i], mixed[i], preferred_element_type=F32)
                + jnp.dot(high[i], mixed_low[i], preferred_element_type=F32)
                + ridge * direction[i]
                for i in each
            ]
            step_size = [norm_now[i] / row_sum(direction[i] * mapped[i]) for i in each]
            answer = [
                step_size[i] * direction[i]
                if turn == 0
                else answer[i] + step_size[i] * direction[i]
                for i in each
            ]
            if turn + 1 < ITERS:
                residual = [residual[i] - step_size[i] * mapped[i] for i in each]
                norm_next = [row_sum(r * r) for r in residual]
                direction = [
                    residual[i] + norm_next[i] / norm_now[i] * direction[i] for i in each
                ]
                norm_now = norm_next
        for i in each:
            solved[kind, i] = answer[i]

    b_done = {}

    def state_cols(place):
        return pl.ds(pl.multiple_of(place * SPAN, SPAN), SPAN)

    def read(kind):
        gain = pick_row(gain_ref[...], me)
        here = token_rows(kind)
        for i in range(inner):
            o = i + 1
            b = block_of(kind, i)
            answer = solved[kind, i]
            corr = correlate(answer, b)
            left = jnp.concatenate(
                [
                    (carried[b, here, :] * answer).astype(BF16),
                    (corr * weights[b, here, :]).astype(BF16),
                ],
                axis=1,
            )
            mixed = jnp.concatenate([start_state(1, b).astype(BF16), vb[block_rows(b), :]], axis=0)
            raw = jnp.dot(left, mixed, preferred_element_type=F32)
            scale = lax.rsqrt(jnp.mean(raw * raw, axis=-1, keepdims=True) + EPSILON)
            normed = (raw * scale * gain).astype(BF16)
            if o == inner:
                readout[kind, :, state_cols(me)] = normed
            else:
                sending[kind, i] = normed
                copy = remote(
                    sending.at[kind, i], readout.at[kind, :, state_cols(me)],
                    b_send.at[kind, o], b_recv.at[kind, o], plane[3](shift_plane(o, 1)),
                )
                copy.start()
                pending.append(copy.wait_send)
                back = shift_plane(o, -1)
                b_done[kind, o] = remote(
                    sending.at[kind, i], readout.at[kind, :, state_cols(back)],
                    b_send.at[kind, o], b_recv.at[kind, o], plane[3](back),
                ).wait_recv

    def wait_readout(kind):
        for o in range(1, inner):
            b_done.pop((kind, o))()

    tiles = half // TILE
    far, near_1, near_2, _ = chunks

    def tile_cols(side, c):
        return slice(side * half + c * TILE, side * half + (c + 1) * TILE)

    def project(kind, side, c):
        return jnp.dot(
            readout[kind], wv[:, tile_cols(side, c)], preferred_element_type=F32
        )

    def result_copy(i, c, kind, side, landing, peer):
        return remote(
            partial.at[kind, :, tile_cols(side, c)], landing.at[:, tile_cols(0, c)],
            r_send.at[i, c], r_recv.at[i, c], (s, peer),
        )

    results = [
        lambda c: result_copy(0, c, 0, 0, relay_a, near_1),
        lambda c: result_copy(1, c, 0, 1, relay_b, near_2),
        lambda c: result_copy(2, c, 1, 0, n1_a, near_1),
        lambda c: result_copy(3, c, 1, 1, n1_b, near_1),
        lambda c: result_copy(4, c, 2, 1, n2_b, near_2),
        lambda c: result_copy(5, c, 2, 0, n2_a, near_2),
    ]

    def send_tile(i, c, kind, side, value):
        partial[kind, :, tile_cols(side, c)] = value.astype(BF16)
        results[i](c).start()

    for kind in range(3):
        if kind > 0:
            wait_queries(kind)
        solve(kind)
        read(kind)
    w_copy.wait()
    wait_readout(0)
    for c in range(tiles):
        send_tile(0, c, 0, 0, project(0, 0, c))
        send_tile(1, c, 0, 1, project(0, 1, c))
    wait_readout(1)
    for c in range(tiles):
        send_tile(2, c, 1, 0, project(1, 0, c))
    wait_readout(2)
    for c in range(tiles):
        send_tile(4, c, 2, 1, project(2, 1, c))
    wait_queries(3)
    solve(3)
    read(3)
    for c in range(tiles):
        results[1](c).wait_recv()
        send_tile(3, c, 1, 1, project(1, 1, c) + relay_b[:, tile_cols(0, c)].astype(F32))
        results[0](c).wait_recv()
        send_tile(5, c, 2, 0, project(2, 0, c) + relay_a[:, tile_cols(0, c)].astype(F32))
    wait_readout(3)
    for c in range(tiles):
        for side in range(2):
            own[:, tile_cols(side, c)] = project(3, side, c)

    for c in range(tiles):
        for side, (i1, from_1), (i2, from_2) in (
            (0, (2, n1_a), (5, n2_a)),
            (1, (3, n1_b), (4, n2_b)),
        ):
            results[i1](c).wait_recv()
            results[i2](c).wait_recv()
            cols = tile_cols(side, c)
            out_ref[:, cols] = (
                own[:, cols]
                + from_1[:, tile_cols(0, c)].astype(F32)
                + from_2[:, tile_cols(0, c)].astype(F32)
            ).astype(BF16)

    for result in results:
        for c in range(tiles):
            result(c).wait_send()
    for fn in pending:
        fn()


def body(planes, inner, query_rows, key_rows, value_rows, log_decay, regularizer, norm_gain, out_weight):
    ring = lax.axis_size("head")
    rows, model = query_rows.shape
    heads = regularizer.shape[0]
    tokens = rows * ring * inner
    blocks = tokens // SPAN
    half = model // 2
    piece = SPAN // planes
    vm = pltpu.VMEM
    dma = pltpu.SemaphoreType.DMA
    scratch = [
        vm((inner,) + log_decay.shape, F32),
        pltpu.SMEM(regularizer.shape, F32),
        vm(norm_gain.shape, F32),
        vm((tokens, SPAN), BF16),
        vm((tokens, SPAN), BF16),
        vm((tokens, SPAN), BF16),
        vm((heads * SPAN, model), BF16),
        vm((blocks, SPAN, SPAN), F32),
        vm((blocks, SPAN, SPAN), F32),
        vm((blocks, SPAN, SPAN), F32),
        vm((blocks, 8, SPAN), F32),
        vm((blocks, 8, SPAN), F32),
        vm((8, SPAN), F32),
        vm((blocks, SPAN, SPAN), BF16),
        vm((blocks, SPAN, SPAN), BF16),
        vm((blocks, SPAN, SPAN), BF16),
        vm((blocks, SPAN, SPAN), F32),
        vm((2, blocks, SPAN, SPAN), F32),
        vm((planes, 4 * piece, SPAN), BF16),
        vm((planes, 4 * piece, SPAN), BF16),
        vm((planes, 3 * piece, SPAN), BF16),
        vm((planes, 3 * piece, SPAN), BF16),
        vm((2, SPAN, SPAN), F32),
        vm((ring, inner, rows, SPAN), F32),
        vm((ring, inner - 1, rows, SPAN), BF16),
        vm((ring, rows, heads * SPAN), BF16),
        vm((rows, model), F32),
        vm((ring - 1, rows, model), BF16),
    ]
    scratch += [vm((rows, half), BF16)] * 6
    scratch += [dma((7,))] + [dma((inner,))] * 2 + [dma((3, inner * ring))] * 2
    scratch += [dma((planes,))] * 4 + [dma((ring, inner))] * 2
    scratch += [dma((6, half // TILE))] * 2
    in_hbm = pl.BlockSpec(memory_space=pltpu.HBM)
    return pl.pallas_call(
        functools.partial(kernel, planes, inner, ring),
        out_shape=jax.ShapeDtypeStruct((rows, model), BF16),
        in_specs=[in_hbm] * 7,
        out_specs=pl.BlockSpec(memory_space=pltpu.VMEM),
        scratch_shapes=scratch,
        compiler_params=pltpu.CompilerParams(
            collective_id=0, has_side_effects=True, vmem_limit_bytes=63 * 1024 * 1024
        ),
    )(query_rows, key_rows, value_rows, log_decay, regularizer, norm_gain, out_weight)


def solution(mesh):
    placed = (
        P(("seq", "head"), None),
        P(("seq", "head"), None),
        P(("seq", "head"), None),
        P("head", "seq"),
        P("head"),
        P("head", None),
        P("head", None),
    )
    inner = 8
    planes = mesh.shape["seq"] // inner
    return jax.shard_map(
        functools.partial(body, planes, inner), mesh=mesh, in_specs=placed,
        out_specs=P(("seq", "head"), None), check_vma=False,
    )
```

```python
import functools

import jax
import jax.numpy as jnp
from jax import lax
from jax.experimental import pallas as pl
from jax.experimental.pallas import tpu as pltpu
from jax.sharding import PartitionSpec as P

SPAN = 128
ITERS = 4
EPSILON = 1e-06
TILE = 512
BATCH = 2
MESH = pl.DeviceIdType.MESH
HIGHEST = lax.Precision.HIGHEST
F32 = jnp.float32
BF16 = jnp.bfloat16
ROWS_BY_ROWS = (((1,), (1,)), ((), ()))
COLS_BY_COLS = (((0,), (0,)), ((), ()))


def kernel(
    planes, inner, ring,
    q_hbm, k_hbm, v_hbm, ld_hbm, reg_hbm, gain_hbm, w_hbm, out_ref,
    ld_plane, reg_ref, gain_ref, qb, kb, vb, wv, weights, carried, tails, leave, enter, dec_total,
    kpair, tailed, terms, before, z_to, z_in, z_out, z_back, z_state,
    solved, sending, readout, own, partial,
    relay_a, relay_b, n1_a, n1_b, n2_a, n2_b,
    local_sem, ld_send, ld_recv, g_send, g_recv,
    z_send, z_recv, zb_send, zb_recv, b_send, b_recv, r_send, r_recv,
):
    s = lax.axis_index("seq")
    x = lax.axis_index("head")
    z = lax.div(s, inner)
    me = lax.rem(s, inner)
    rows = q_hbm.shape[0]
    blocks = kpair.shape[0]
    per_device = blocks // inner
    half = w_hbm.shape[1] // 2
    pending = []

    def loop(lo, hi, fn):
        def step(i, carry):
            fn(i)
            return carry
        lax.fori_loop(lo, hi, step, 0)

    def shift_plane(o, sign):
        return lax.rem(me + inner + sign * o, inner)

    def shift_z(o, sign):
        return lax.rem(z + planes + sign * o, planes)

    def shift_group(o, sign):
        over = lax.div(o, ring)
        along = lax.rem(o, ring)
        return (
            lax.rem(me + inner + sign * over, inner), lax.rem(x + ring + sign * along, ring)
        )

    def shift_far(mask):
        return lambda o, sign: (lax.rem(me + inner + sign * o, inner), x ^ mask)

    def in_group(peer):
        return (z * inner + peer[0], peer[1])

    plane = (1, inner, shift_plane, lambda peer: (z * inner + peer, x))
    column = (1, planes, shift_z, lambda peer: (peer * inner + me, x))
    group = (1, inner * ring, shift_group, in_group)
    kinds = [(0 if mask else 1, inner, shift_far(mask), in_group) for mask in (2, 3, 1, 0)]

    def remote(src, dst, send, recv, device):
        return pltpu.make_async_remote_copy(
            src_ref=src, dst_ref=dst, send_sem=send, recv_sem=recv,
            device_id=device, device_id_type=MESH,
        )

    def exchange(partners, make_pair, send, recv, here, later=False):
        first, count, shift, device = partners

        def copy(o, sign):
            peer = shift(o, sign)
            src, dst = make_pair(peer, here) if sign == 1 else make_pair(here, peer)
            return remote(src, dst, send(o), recv(o), device(peer))

        pending.append(lambda: loop(first, count, lambda o: copy(o, 1).wait_send()))
        if later:
            return (lambda o: copy(o, 1).start()), (lambda o: copy(o, -1).wait_recv())
        loop(first, count, lambda o: copy(o, 1).start())
        return lambda o: copy(o, -1).wait_recv()

    def all_of(partners, got):
        loop(partners[0], partners[1], got)

    small = [
        pltpu.make_async_copy(src, dst, local_sem.at[i])
        for i, (src, dst) in enumerate(
            ((ld_hbm, ld_plane.at[me]), (reg_hbm, reg_ref), (gain_hbm, gain_ref))
        )
    ]
    for copy in small:
        copy.start()

    barrier = pltpu.get_barrier_semaphore()
    for _, count, shift, device in (group, column):
        loop(
            1, count,
            lambda o, shift=shift, device=device: pl.semaphore_signal(
                barrier, inc=1, device_id=device(shift(o, 1)), device_id_type=MESH
            ),
        )
    pl.semaphore_wait(barrier, inner * ring - 1 + planes - 1)

    got_ld = exchange(
        plane, lambda to, frm: (ld_hbm, ld_plane.at[frm]),
        lambda o: ld_send.at[o], lambda o: ld_recv.at[o], me,
    )

    def slot(place):
        return pl.ds(pl.multiple_of((place[0] * ring + place[1]) * rows, rows), rows)

    def head_cols(place):
        return pl.ds(pl.multiple_of((place[1] * inner + place[0]) * SPAN, SPAN), SPAN)

    got_group = []
    for i, (src_hbm, dst_buf) in enumerate(((k_hbm, kb), (v_hbm, vb), (q_hbm, qb))):
        def make(to, frm, src_hbm=src_hbm, dst_buf=dst_buf):
            return src_hbm.at[:, head_cols(to)], dst_buf.at[slot(frm), :]

        mine = pltpu.make_async_copy(*make((me, x), (me, x)), local_sem.at[3 + i])
        mine.start()
        parts = [group] if i < 2 else kinds
        moves = [
            exchange(
                part, make,
                lambda o, i=i, at=n * inner: g_send.at[i, at + o],
                lambda o, i=i, at=n * inner: g_recv.at[i, at + o],
                (me, x), later=True,
            )
            for n, part in enumerate(parts)
        ]
        got_group.append((mine, moves))

    def go_group(i, n=0):
        part = group if i < 2 else kinds[n]
        loop(part[0], part[1], got_group[i][1][n][0])

    go_group(0)
    go_group(1)
    w_copy = pltpu.make_async_copy(w_hbm, wv, local_sem.at[6])

    def pick_row(table, i):
        place = lax.broadcasted_iota(jnp.int32, table.shape, 0)
        return jnp.sum(jnp.where(place == i, table, 0.0), axis=0, keepdims=True)

    row_id = lax.broadcasted_iota(jnp.int32, (SPAN, SPAN), 0)
    col_id = lax.broadcasted_iota(jnp.int32, (SPAN, SPAN), 1)
    causal = row_id >= col_id
    for copy in small:
        copy.wait()
    all_of(plane, got_ld)

    def down(row):
        return jnp.transpose(jnp.broadcast_to(row, (SPAN, SPAN)))

    sums = lax.dot_general(
        jnp.concatenate(
            [
                pick_row(ld_plane[b // per_device][:, (b % per_device) * SPAN:(b % per_device + 1) * SPAN], me)
                for b in range(blocks)
            ],
            axis=0,
        ),
        jnp.where(causal, 1.0, 0.0).astype(F32),
        ROWS_BY_ROWS, precision=HIGHEST, preferred_element_type=F32,
    )
    total = jnp.zeros((8, SPAN), F32)
    for b in range(blocks):
        row = sums[b:b + 1, :]
        last = jnp.broadcast_to(row[:, SPAN - 1:SPAN], (8, SPAN))
        enter[b] = jnp.exp(total)
        total = total + last
        cum = down(row)
        tails[b] = jnp.exp(last[0:1, :] - cum)
        weights[b] = jnp.where(causal, jnp.exp(jnp.minimum(cum - row, 0.0)), 0.0)
        carried[b] = jnp.exp(cum)
        leave[b] = jnp.exp(last)
    dec_total[...] = total

    def split(value):
        high = value.astype(BF16)
        return high, (value - high.astype(F32)).astype(BF16)

    def block_rows(b):
        return pl.ds(pl.multiple_of(b * SPAN, SPAN), SPAN)

    def plane_states(t):
        mine, ((_, got),) = got_group[t]

        def states(overs):
            bs = [
                lax.rem(me + inner - over, inner) * per_device + n
                for over in overs
                for n in range(per_device)
            ]
            if t == 0:
                keys = [kb[block_rows(b), :].astype(F32) for b in bs]
                scales = [
                    lax.rsqrt(jnp.mean(key * key, axis=-1, keepdims=True) + EPSILON)
                    * SPAN ** -0.5
                    for key in keys
                ]
                normed = [key * scale for key, scale in zip(keys, scales)]
                pairs = [split(value) for value in normed]
                lefts = [split(tails[b] * value) for b, value in zip(bs, normed)]
                products = [
                    lax.dot_general(
                        jnp.concatenate([left[0], left[1], left[0]], axis=0),
                        jnp.concatenate([pair[0], pair[0], pair[1]], axis=0),
                        COLS_BY_COLS, preferred_element_type=F32,
                    )
                    for left, pair in zip(lefts, pairs)
                ]
                for b, pair, left in zip(bs, pairs, lefts):
                    kpair[b, :SPAN, :], kpair[b, SPAN:, :] = pair
                    tailed[b] = left[0]
            else:
                products = [
                    lax.dot_general(
                        tailed[b], vb[block_rows(b), :], COLS_BY_COLS,
                        preferred_element_type=F32,
                    )
                    for b in bs
                ]
            for b, product in zip(bs, products):
                terms[b] = product

        def batch(i):
            if isinstance(i, int):
                mine.wait()
                loop(1, BATCH * ring, got)
            else:
                loop(i * BATCH * ring, (i + 1) * BATCH * ring, got)
            states([i * BATCH + n for n in range(BATCH)])

        batch(0)
        loop(1, inner // BATCH, batch)
        plane_total = jnp.zeros((SPAN, SPAN), F32)
        for b in range(blocks):
            before[t, b] = plane_total
            plane_total = leave[b][0:1, :] * plane_total + terms[b]
        for i in range(planes):
            rows_of = plane_total[i * piece:(i + 1) * piece, :]
            if t == 0:
                z_to[i, 0:piece, :], z_to[i, piece:2 * piece, :] = split(rows_of)
            else:
                z_to[i, 2 * piece:3 * piece, :] = rows_of.astype(BF16)

    piece = SPAN // planes

    def send_z():
        rest = dec_total[0:1, :]
        terms_of = []
        for _ in range(3):
            term = rest.astype(BF16)
            terms_of.append(jnp.broadcast_to(term.astype(F32), (8, SPAN)))
            rest = rest - term.astype(F32)
        place = lax.broadcasted_iota(jnp.int32, (piece, SPAN), 0)
        packed = jnp.zeros((piece, SPAN), F32)
        for i, term in enumerate(terms_of):
            packed = jnp.where(place == i, term[0:1, :], packed)
        packed = packed.astype(BF16)
        for i in range(planes):
            z_to[i, 3 * piece:4 * piece, :] = packed
        got = exchange(
            column, lambda to, frm: (z_to.at[to], z_in.at[frm]),
            lambda o: z_send.at[o], lambda o: z_recv.at[o], z,
        )
        z_in[z] = z_to[z]
        return got

    def z_prefix():
        gram = jnp.zeros((piece, SPAN), F32)
        memory = gram
        for i in range(planes):
            z_out[i, 0:piece, :], z_out[i, piece:2 * piece, :] = split(gram)
            z_out[i, 2 * piece:3 * piece, :] = memory.astype(BF16)
            if i + 1 < planes:
                arrived = z_in[i].astype(F32)
                tail = arrived[3 * piece:4 * piece, :]
                decay = jnp.exp(tail[0:1, :] + tail[1:2, :] + tail[2:3, :])
                gram = decay * gram + (arrived[0:piece, :] + arrived[piece:2 * piece, :])
                memory = decay * memory + arrived[2 * piece:3 * piece, :]

    def send_z_back():
        got = exchange(
            column, lambda to, frm: (z_out.at[to], z_back.at[frm]),
            lambda o: zb_send.at[o], lambda o: zb_recv.at[o], z,
        )
        z_back[z] = z_out[z]
        return got

    def collect():
        for i in range(planes):
            arrived = z_back[i].astype(F32)
            here = slice(i * piece, (i + 1) * piece)
            z_state[0, here, :] = arrived[0:piece, :] + arrived[piece:2 * piece, :]
            z_state[1, here, :] = arrived[2 * piece:3 * piece, :]

    def wait_queries(kind):
        mine, moves = got_group[2]
        if kind == 3:
            mine.wait()
        all_of(kinds[kind], moves[kind][1])

    plane_states(0)
    plane_states(1)
    got_z = send_z()
    for kind in range(4):
        go_group(2, kind)
    all_of(column, got_z)
    z_prefix()
    got_zb = send_z_back()
    w_copy.start()
    wait_queries(0)
    all_of(column, got_zb)
    collect()

    def start_state(t, b):
        return enter[b][0:1, :] * z_state[t] + before[t, b]

    def row_sum(a):
        return jnp.sum(a, axis=-1, keepdims=True)

    chunks = [x ^ mask for mask in (2, 3, 1, 0)]

    def member(i):
        return lax.rem(me + 1 + i, inner)

    def block_of(kind, i):
        return member(i) * per_device + lax.div(chunks[kind], ring // per_device)

    def token_rows(kind):
        return pl.ds(
            pl.multiple_of(lax.rem(chunks[kind], ring // per_device) * rows, rows), rows
        )

    def correlate(vector, b):
        return add_terms(
            lax.dot_general(
                jnp.concatenate(split(vector), axis=0), kpair[b], ROWS_BY_ROWS,
                preferred_element_type=F32,
            )
        )

    def add_terms(products):
        high, low = products[:rows, :], products[rows:, :]
        return high[:, :SPAN] + (high[:, SPAN:] + low[:, :SPAN])

    def solve(kind):
        each = range(inner)
        bs = [block_of(kind, i) for i in each]
        here = token_rows(kind)
        ridge = reg_ref[me]
        states = [split(start_state(0, b)) for b in bs]
        mixed = [
            jnp.concatenate(
                [
                    jnp.concatenate(states[i], axis=1),
                    jnp.concatenate([kpair[bs[i], :SPAN, :], kpair[bs[i], SPAN:, :]], axis=1),
                ],
                axis=0,
            )
            for i in each
        ]
        direction = [qb[slot((member(i), chunks[kind])), :].astype(F32) for i in each]
        residual = list(direction)
        answer = [None] * inner
        norm_now = [row_sum(r * r) for r in residual]
        for turn in range(ITERS):
            corr = [correlate(direction[i], bs[i]) for i in each]
            from_state = [split(carried[bs[i], here, :] * direction[i]) for i in each]
            from_block = [split(corr[i] * weights[bs[i], here, :]) for i in each]
            both = [
                jnp.concatenate(
                    [
                        jnp.concatenate([from_state[i][n], from_block[i][n]], axis=1)
                        for n in range(2)
                    ],
                    axis=0,
                )
                for i in each
            ]
            mapped = [
                add_terms(jnp.dot(both[i], mixed[i], preferred_element_type=F32))
                + ridge * direction[i]
                for i in each
            ]
            step_size = [norm_now[i] / row_sum(direction[i] * mapped[i]) for i in each]
            answer = [
                step_size[i] * direction[i]
                if turn == 0
                else answer[i] + step_size[i] * direction[i]
                for i in each
            ]
            if turn + 1 < ITERS:
                residual = [residual[i] - step_size[i] * mapped[i] for i in each]
                norm_next = [row_sum(r * r) for r in residual]
                direction = [
                    residual[i] + norm_next[i] / norm_now[i] * direction[i] for i in each
                ]
                norm_now = norm_next
        for i in each:
            solved[kind, i] = answer[i]

    b_done = {}

    def state_cols(place):
        return pl.ds(pl.multiple_of(place * SPAN, SPAN), SPAN)

    def read(kind):
        gain = pick_row(gain_ref[...], me)
        here = token_rows(kind)
        each = range(inner)
        bs = [block_of(kind, i) for i in each]
        answers = [solved[kind, i] for i in each]
        corr = [correlate(answers[i], bs[i]) for i in each]
        left = [
            jnp.concatenate(
                [
                    (carried[bs[i], here, :] * answers[i]).astype(BF16),
                    (corr[i] * weights[bs[i], here, :]).astype(BF16),
                ],
                axis=1,
            )
            for i in each
        ]
        mixed = [
            jnp.concatenate([start_state(1, b).astype(BF16), vb[block_rows(b), :]], axis=0)
            for b in bs
        ]
        raws = [jnp.dot(left[i], mixed[i], preferred_element_type=F32) for i in each]
        scales = [
            lax.rsqrt(jnp.mean(raw * raw, axis=-1, keepdims=True) + EPSILON) for raw in raws
        ]
        results_of = [(raws[i] * scales[i] * gain).astype(BF16) for i in each]
        for i in each:
            o = i + 1
            normed = results_of[i]
            if o == inner:
                readout[kind, :, state_cols(me)] = normed
            else:
                sending[kind, i] = normed
        for i in range(inner - 1):
            o = i + 1
            copy = remote(
                sending.at[kind, i], readout.at[kind, :, state_cols(me)],
                b_send.at[kind, o], b_recv.at[kind, o], plane[3](shift_plane(o, 1)),
            )
            copy.start()
            pending.append(copy.wait_send)
            back = shift_plane(o, -1)
            b_done[kind, o] = remote(
                sending.at[kind, i], readout.at[kind, :, state_cols(back)],
                b_send.at[kind, o], b_recv.at[kind, o], plane[3](back),
            ).wait_recv

    def wait_readout(kind):
        for o in range(1, inner):
            b_done.pop((kind, o))()

    tiles = half // TILE
    far, near_1, near_2, _ = chunks

    def tile_cols(side, c):
        return slice(side * half + c * TILE, side * half + (c + 1) * TILE)

    def project(kind, side, c):
        return jnp.dot(
            readout[kind], wv[:, tile_cols(side, c)], preferred_element_type=F32
        )

    def result_copy(i, c, kind, side, landing, peer):
        return remote(
            partial.at[kind, :, tile_cols(side, c)], landing.at[:, tile_cols(0, c)],
            r_send.at[i, c], r_recv.at[i, c], (s, peer),
        )

    results = [
        lambda c: result_copy(0, c, 0, 0, relay_a, near_1),
        lambda c: result_copy(1, c, 0, 1, relay_b, near_2),
        lambda c: result_copy(2, c, 1, 0, n1_a, near_1),
        lambda c: result_copy(3, c, 1, 1, n1_b, near_1),
        lambda c: result_copy(4, c, 2, 1, n2_b, near_2),
        lambda c: result_copy(5, c, 2, 0, n2_a, near_2),
    ]

    def send_tiles(cs, batch):
        for c in cs:
            values = [project(kind, side, c) for _, kind, side in batch]
            for (_, kind, side), value in zip(batch, values):
                partial[kind, :, tile_cols(side, c)] = value.astype(BF16)
        for c in cs:
            for i, _, _ in batch:
                results[i](c).start()

    for kind in range(3):
        if kind > 0:
            wait_queries(kind)
        solve(kind)
        read(kind)
    w_copy.wait()
    wait_readout(0)
    for c in range(0, tiles, 2):
        send_tiles((c, c + 1), ((0, 0, 0), (1, 0, 1)))
    wait_readout(1)
    send_tiles(range(tiles), ((2, 1, 0),))
    wait_readout(2)
    send_tiles(range(tiles), ((4, 2, 1),))
    wait_queries(3)
    solve(3)
    read(3)
    for c in range(tiles):
        here = tile_cols(0, c)
        values = project(1, 1, c), project(2, 0, c)
        own[:, here], own[:, tile_cols(1, c)] = values
    for c in range(tiles):
        results[1](c).wait_recv()
        results[0](c).wait_recv()
        here = tile_cols(0, c)
        there = tile_cols(1, c)
        partial[1, :, there] = (own[:, here] + relay_b[:, here].astype(F32)).astype(BF16)
        partial[2, :, here] = (own[:, there] + relay_a[:, here].astype(F32)).astype(BF16)
        results[3](c).start()
        results[5](c).start()
    wait_readout(3)
    for c in range(tiles):
        for side in range(2):
            own[:, tile_cols(side, c)] = project(3, side, c)

    for c in range(tiles):
        for side, (i1, from_1), (i2, from_2) in (
            (0, (2, n1_a), (5, n2_a)),
            (1, (3, n1_b), (4, n2_b)),
        ):
            results[i1](c).wait_recv()
            results[i2](c).wait_recv()
            cols = tile_cols(side, c)
            out_ref[:, cols] = (
                own[:, cols]
                + from_1[:, tile_cols(0, c)].astype(F32)
                + from_2[:, tile_cols(0, c)].astype(F32)
            ).astype(BF16)

    for result in results:
        for c in range(tiles):
            result(c).wait_send()
    for fn in pending:
        fn()


def body(planes, inner, query_rows, key_rows, value_rows, log_decay, regularizer, norm_gain, out_weight):
    ring = lax.axis_size("head")
    rows, model = query_rows.shape
    heads = regularizer.shape[0]
    tokens = rows * ring * inner
    blocks = tokens // SPAN
    half = model // 2
    piece = SPAN // planes
    vm = pltpu.VMEM
    dma = pltpu.SemaphoreType.DMA
    scratch = [
        vm((inner,) + log_decay.shape, F32),
        pltpu.SMEM(regularizer.shape, F32),
        vm(norm_gain.shape, F32),
        vm((tokens, SPAN), BF16),
        vm((tokens, SPAN), BF16),
        vm((tokens, SPAN), BF16),
        vm((heads * SPAN, model), BF16),
        vm((blocks, SPAN, SPAN), F32),
        vm((blocks, SPAN, SPAN), F32),
        vm((blocks, SPAN, SPAN), F32),
        vm((blocks, 8, SPAN), F32),
        vm((blocks, 8, SPAN), F32),
        vm((8, SPAN), F32),
        vm((blocks, 2 * SPAN, SPAN), BF16),
        vm((blocks, SPAN, SPAN), BF16),
        vm((blocks, SPAN, SPAN), F32),
        vm((2, blocks, SPAN, SPAN), F32),
        vm((planes, 4 * piece, SPAN), BF16),
        vm((planes, 4 * piece, SPAN), BF16),
        vm((planes, 3 * piece, SPAN), BF16),
        vm((planes, 3 * piece, SPAN), BF16),
        vm((2, SPAN, SPAN), F32),
        vm((ring, inner, rows, SPAN), F32),
        vm((ring, inner - 1, rows, SPAN), BF16),
        vm((ring, rows, heads * SPAN), BF16),
        vm((rows, model), F32),
        vm((ring - 1, rows, model), BF16),
    ]
    scratch += [vm((rows, half), BF16)] * 6
    scratch += [dma((7,))] + [dma((inner,))] * 2 + [dma((3, inner * ring))] * 2
    scratch += [dma((planes,))] * 4 + [dma((ring, inner))] * 2
    scratch += [dma((6, half // TILE))] * 2
    in_hbm = pl.BlockSpec(memory_space=pltpu.HBM)
    return pl.pallas_call(
        functools.partial(kernel, planes, inner, ring),
        out_shape=pltpu.VMEM((rows, model), BF16),
        in_specs=[in_hbm] * 7,
        out_specs=pl.BlockSpec(memory_space=pltpu.VMEM),
        scratch_shapes=scratch,
        compiler_params=pltpu.CompilerParams(
            collective_id=0, has_side_effects=True, vmem_limit_bytes=60 * 1024 * 1024
        ),
    )(query_rows, key_rows, value_rows, log_decay, regularizer, norm_gain, out_weight)


def solution(mesh):
    placed = (
        P(("seq", "head"), None),
        P(("seq", "head"), None),
        P(("seq", "head"), None),
        P("head", "seq"),
        P("head"),
        P("head", None),
        P("head", None),
    )
    inner = 8
    planes = mesh.shape["seq"] // inner
    return jax.shard_map(
        functools.partial(body, planes, inner), mesh=mesh, in_specs=placed,
        out_specs=P(("seq", "head"), None), check_vma=False,
    )
```

```python
import functools

import jax
import jax.numpy as jnp
from jax import lax
from jax.experimental import pallas as pl
from jax.experimental.pallas import tpu as pltpu
from jax.sharding import PartitionSpec as P

SPAN = 128
ITERS = 4
EPSILON = 1e-06
TILE = 512
BATCH = 2
MESH = pl.DeviceIdType.MESH
HIGHEST = lax.Precision.HIGHEST
F32 = jnp.float32
BF16 = jnp.bfloat16
ROWS_BY_ROWS = (((1,), (1,)), ((), ()))
COLS_BY_COLS = (((0,), (0,)), ((), ()))


def kernel(
    planes, inner, ring,
    q_hbm, k_hbm, v_hbm, ld_hbm, reg_hbm, gain_hbm, w_hbm, out_ref,
    ld_plane, reg_ref, gain_ref, qb, kb, vb, wv, weights, carried, tails, leave, enter, to_end, dec_total,
    kpair, tailed, terms, before, z_to, z_in, z_out, z_back, z_state,
    solved, sending, readout, own, partial,
    relay_a, relay_b, n1_a, n1_b, n2_a, n2_b,
    local_sem, ld_send, ld_recv, g_send, g_recv,
    z_send, z_recv, zb_send, zb_recv, b_send, b_recv, r_send, r_recv,
):
    s = lax.axis_index("seq")
    x = lax.axis_index("head")
    z = lax.div(s, inner)
    me = lax.rem(s, inner)
    rows = q_hbm.shape[0]
    blocks = kpair.shape[0]
    per_device = blocks // inner
    half = w_hbm.shape[1] // 2
    pending = []

    def loop(lo, hi, fn):
        def step(i, carry):
            fn(i)
            return carry
        lax.fori_loop(lo, hi, step, 0)

    def shift_plane(o, sign):
        return lax.rem(me + inner + sign * o, inner)

    def shift_z(o, sign):
        return lax.rem(z + planes + sign * o, planes)

    def shift_group(o, sign):
        over = lax.div(o, ring)
        along = lax.rem(o, ring)
        return (
            lax.rem(me + inner + sign * over, inner), lax.rem(x + ring + sign * along, ring)
        )

    def shift_far(mask):
        return lambda o, sign: (lax.rem(me + inner + sign * o, inner), x ^ mask)

    def in_group(peer):
        return (z * inner + peer[0], peer[1])

    plane = (1, inner, shift_plane, lambda peer: (z * inner + peer, x))
    column = (1, planes, shift_z, lambda peer: (peer * inner + me, x))
    group = (1, inner * ring, shift_group, in_group)
    kinds = [(0 if mask else 1, inner, shift_far(mask), in_group) for mask in (2, 3, 1, 0)]

    def remote(src, dst, send, recv, device):
        return pltpu.make_async_remote_copy(
            src_ref=src, dst_ref=dst, send_sem=send, recv_sem=recv,
            device_id=device, device_id_type=MESH,
        )

    def exchange(partners, make_pair, send, recv, here, later=False):
        first, count, shift, device = partners

        def copy(o, sign):
            peer = shift(o, sign)
            src, dst = make_pair(peer, here) if sign == 1 else make_pair(here, peer)
            return remote(src, dst, send(o), recv(o), device(peer))

        pending.append(lambda: loop(first, count, lambda o: copy(o, 1).wait_send()))
        if later:
            return (lambda o: copy(o, 1).start()), (lambda o: copy(o, -1).wait_recv())
        for o in range(first, count):
            copy(o, 1).start()
        return lambda o: copy(o, -1).wait_recv()

    def all_of(partners, got):
        loop(partners[0], partners[1], got)

    small = [
        pltpu.make_async_copy(src, dst, local_sem.at[i])
        for i, (src, dst) in enumerate(
            ((ld_hbm, ld_plane.at[me]), (reg_hbm, reg_ref), (gain_hbm, gain_ref))
        )
    ]
    for copy in small:
        copy.start()

    barrier = pltpu.get_barrier_semaphore()
    for _, count, shift, device in (group, column):
        loop(
            1, count,
            lambda o, shift=shift, device=device: pl.semaphore_signal(
                barrier, inc=1, device_id=device(shift(o, 1)), device_id_type=MESH
            ),
        )
    pl.semaphore_wait(barrier, inner * ring - 1 + planes - 1)

    got_ld = exchange(
        plane, lambda to, frm: (ld_hbm, ld_plane.at[frm]),
        lambda o: ld_send.at[o], lambda o: ld_recv.at[o], me,
    )

    def slot(place):
        return pl.ds(pl.multiple_of((place[0] * ring + place[1]) * rows, rows), rows)

    def head_cols(place):
        return pl.ds(pl.multiple_of((place[1] * inner + place[0]) * SPAN, SPAN), SPAN)

    got_group = []
    for i, (src_hbm, dst_buf) in enumerate(((k_hbm, kb), (v_hbm, vb), (q_hbm, qb))):
        def make(to, frm, src_hbm=src_hbm, dst_buf=dst_buf):
            return src_hbm.at[:, head_cols(to)], dst_buf.at[slot(frm), :]

        mine = pltpu.make_async_copy(*make((me, x), (me, x)), local_sem.at[3 + i])
        mine.start()
        parts = [group] if i < 2 else kinds
        moves = [
            exchange(
                part, make,
                lambda o, i=i, at=n * inner: g_send.at[i, at + o],
                lambda o, i=i, at=n * inner: g_recv.at[i, at + o],
                (me, x), later=True,
            )
            for n, part in enumerate(parts)
        ]
        got_group.append((mine, moves))

    def go_group(i, n=0):
        part = group if i < 2 else kinds[n]
        loop(part[0], part[1], got_group[i][1][n][0])

    go_group(0)
    go_group(1)
    w_copy = pltpu.make_async_copy(w_hbm, wv, local_sem.at[6])

    def pick_row(table, i):
        place = lax.broadcasted_iota(jnp.int32, table.shape, 0)
        return jnp.sum(jnp.where(place == i, table, 0.0), axis=0, keepdims=True)

    row_id = lax.broadcasted_iota(jnp.int32, (SPAN, SPAN), 0)
    col_id = lax.broadcasted_iota(jnp.int32, (SPAN, SPAN), 1)
    causal = row_id >= col_id
    for copy in small:
        copy.wait()
    all_of(plane, got_ld)

    def down(row):
        return jnp.transpose(jnp.broadcast_to(row, (SPAN, SPAN)))

    sums = lax.dot_general(
        jnp.concatenate(
            [
                pick_row(ld_plane[b // per_device][:, (b % per_device) * SPAN:(b % per_device + 1) * SPAN], me)
                for b in range(blocks)
            ],
            axis=0,
        ),
        jnp.where(causal, 1.0, 0.0).astype(F32),
        ROWS_BY_ROWS, precision=HIGHEST, preferred_element_type=F32,
    )
    total = jnp.zeros((8, SPAN), F32)
    for b in range(blocks):
        row = sums[b:b + 1, :]
        last = jnp.broadcast_to(row[:, SPAN - 1:SPAN], (8, SPAN))
        enter[b] = jnp.exp(total)
        total = total + last
        to_end[b] = total
        cum = down(row)
        tails[b] = jnp.exp(last[0:1, :] - cum)
        weights[b] = jnp.where(causal, jnp.exp(jnp.minimum(cum - row, 0.0)), 0.0)
        carried[b] = jnp.exp(cum)
        leave[b] = jnp.exp(last)
    dec_total[...] = total
    for b in range(blocks):
        to_end[b] = jnp.exp(total - to_end[b])

    def split(value):
        high = value.astype(BF16)
        return high, (value - high.astype(F32)).astype(BF16)

    def block_rows(b):
        return pl.ds(pl.multiple_of(b * SPAN, SPAN), SPAN)

    def plane_states(t):
        mine, ((_, got),) = got_group[t]

        def states(overs, acc):
            bs = [
                lax.rem(me + inner - over, inner) * per_device + n
                for over in overs
                for n in range(per_device)
            ]
            if t == 0:
                keys = [kb[block_rows(b), :].astype(F32) for b in bs]
                scales = [
                    lax.rsqrt(jnp.mean(key * key, axis=-1, keepdims=True) + EPSILON)
                    * SPAN ** -0.5
                    for key in keys
                ]
                normed = [key * scale for key, scale in zip(keys, scales)]
                pairs = [split(value) for value in normed]
                lefts = [split(tails[b] * value) for b, value in zip(bs, normed)]
                products = [
                    lax.dot_general(
                        jnp.concatenate([left[0], left[1], left[0]], axis=0),
                        jnp.concatenate([pair[0], pair[0], pair[1]], axis=0),
                        COLS_BY_COLS, preferred_element_type=F32,
                    )
                    for left, pair in zip(lefts, pairs)
                ]
                for b, pair, left in zip(bs, pairs, lefts):
                    kpair[b, :SPAN, :], kpair[b, SPAN:, :] = pair
                    tailed[b] = left[0]
            else:
                products = [
                    lax.dot_general(
                        tailed[b], vb[block_rows(b), :], COLS_BY_COLS,
                        preferred_element_type=F32,
                    )
                    for b in bs
                ]
            for b, product in zip(bs, products):
                terms[b] = product
                acc = acc + to_end[b][0:1, :] * product
            return acc

        mine.wait()
        loop(1, BATCH * ring, got)
        plane_total = states(list(range(BATCH)), jnp.zeros((SPAN, SPAN), F32))

        def batch(i, acc):
            loop(i * BATCH * ring, (i + 1) * BATCH * ring, got)
            return states([i * BATCH + n for n in range(BATCH)], acc)

        plane_total = lax.fori_loop(1, inner // BATCH, batch, plane_total)
        for i in range(planes):
            rows_of = plane_total[i * piece:(i + 1) * piece, :]
            if t == 0:
                z_to[i, 0:piece, :], z_to[i, piece:2 * piece, :] = split(rows_of)
            else:
                z_to[i, 2 * piece:3 * piece, :] = rows_of.astype(BF16)

    def block_starts(t):
        acc = jnp.zeros((SPAN, SPAN), F32)
        for b in range(0, blocks, 2):
            factors = leave[b][0:1, :], leave[b + 1][0:1, :]
            added = terms[b], terms[b + 1]
            middle = factors[0] * acc + added[0]
            before[t, b], before[t, b + 1] = acc, middle
            acc = factors[1] * middle + added[1]

    piece = SPAN // planes

    def pack_decay():
        rest = dec_total[0:1, :]
        terms_of = []
        for _ in range(3):
            term = rest.astype(BF16)
            terms_of.append(jnp.broadcast_to(term.astype(F32), (8, SPAN)))
            rest = rest - term.astype(F32)
        place = lax.broadcasted_iota(jnp.int32, (piece, SPAN), 0)
        packed = jnp.zeros((piece, SPAN), F32)
        for i, term in enumerate(terms_of):
            packed = jnp.where(place == i, term[0:1, :], packed)
        packed = packed.astype(BF16)
        for i in range(planes):
            z_to[i, 3 * piece:4 * piece, :] = packed

    def send_z():
        got = exchange(
            column, lambda to, frm: (z_to.at[to], z_in.at[frm]),
            lambda o: z_send.at[o], lambda o: z_recv.at[o], z,
        )
        z_in[z] = z_to[z]
        return got

    def z_prefix():
        arrived = [z_in[i].astype(F32) for i in range(planes - 1)]
        tails_in = [part[3 * piece:4 * piece, :] for part in arrived]
        decays = [jnp.exp(tail[0:1, :] + tail[1:2, :] + tail[2:3, :]) for tail in tails_in]
        grams = [jnp.zeros((piece, SPAN), F32)]
        memories = [grams[0]]
        for part, decay in zip(arrived, decays):
            grams.append(decay * grams[-1] + (part[0:piece, :] + part[piece:2 * piece, :]))
            memories.append(decay * memories[-1] + part[2 * piece:3 * piece, :])
        for i in range(planes):
            z_out[i, 0:piece, :], z_out[i, piece:2 * piece, :] = split(grams[i])
            z_out[i, 2 * piece:3 * piece, :] = memories[i].astype(BF16)

    def send_z_back():
        got = exchange(
            column, lambda to, frm: (z_out.at[to], z_back.at[frm]),
            lambda o: zb_send.at[o], lambda o: zb_recv.at[o], z,
        )
        z_back[z] = z_out[z]
        return got

    def collect():
        arrived = [z_back[i].astype(F32) for i in range(planes)]
        for i in range(planes):
            here = slice(i * piece, (i + 1) * piece)
            z_state[0, here, :] = arrived[i][0:piece, :] + arrived[i][piece:2 * piece, :]
            z_state[1, here, :] = arrived[i][2 * piece:3 * piece, :]

    def wait_queries(kind):
        mine, moves = got_group[2]
        if kind == 3:
            mine.wait()
        all_of(kinds[kind], moves[kind][1])

    pack_decay()
    plane_states(0)
    block_starts(0)
    plane_states(1)
    got_z = send_z()
    go_group(2, 0)
    go_group(2, 1)
    block_starts(1)
    all_of(column, got_z)
    z_prefix()
    got_zb = send_z_back()
    go_group(2, 2)
    go_group(2, 3)
    w_copy.start()
    wait_queries(0)
    all_of(column, got_zb)
    collect()

    def start_state(t, b):
        return enter[b][0:1, :] * z_state[t] + before[t, b]

    def row_sum(a):
        return jnp.sum(a, axis=-1, keepdims=True)

    chunks = [x ^ mask for mask in (2, 3, 1, 0)]

    def member(i):
        return lax.rem(me + 1 + i, inner)

    def block_of(kind, i):
        return member(i) * per_device + lax.div(chunks[kind], ring // per_device)

    def token_rows(kind):
        return pl.ds(
            pl.multiple_of(lax.rem(chunks[kind], ring // per_device) * rows, rows), rows
        )

    def correlate(vector, b):
        return add_terms(
            lax.dot_general(
                jnp.concatenate(split(vector), axis=0), kpair[b], ROWS_BY_ROWS,
                preferred_element_type=F32,
            )
        )

    def add_terms(products):
        high, low = products[:rows, :], products[rows:, :]
        return high[:, :SPAN] + (high[:, SPAN:] + low[:, :SPAN])

    def solve(kind):
        each = range(inner)
        bs = [block_of(kind, i) for i in each]
        here = token_rows(kind)
        ridge = reg_ref[me]
        states = [split(start_state(0, b)) for b in bs]
        mixed = [
            jnp.concatenate(
                [
                    jnp.concatenate(states[i], axis=1),
                    jnp.concatenate([kpair[bs[i], :SPAN, :], kpair[bs[i], SPAN:, :]], axis=1),
                ],
                axis=0,
            )
            for i in each
        ]
        direction = [qb[slot((member(i), chunks[kind])), :].astype(F32) for i in each]
        residual = list(direction)
        answer = [None] * inner
        norm_now = [row_sum(r * r) for r in residual]
        for turn in range(ITERS):
            corr = [correlate(direction[i], bs[i]) for i in each]
            from_state = [split(carried[bs[i], here, :] * direction[i]) for i in each]
            from_block = [split(corr[i] * weights[bs[i], here, :]) for i in each]
            both = [
                jnp.concatenate(
                    [
                        jnp.concatenate([from_state[i][n], from_block[i][n]], axis=1)
                        for n in range(2)
                    ],
                    axis=0,
                )
                for i in each
            ]
            mapped = [
                add_terms(jnp.dot(both[i], mixed[i], preferred_element_type=F32))
                + ridge * direction[i]
                for i in each
            ]
            step_size = [norm_now[i] / row_sum(direction[i] * mapped[i]) for i in each]
            answer = [
                step_size[i] * direction[i]
                if turn == 0
                else answer[i] + step_size[i] * direction[i]
                for i in each
            ]
            if turn + 1 < ITERS:
                residual = [residual[i] - step_size[i] * mapped[i] for i in each]
                norm_next = [row_sum(r * r) for r in residual]
                direction = [
                    residual[i] + norm_next[i] / norm_now[i] * direction[i] for i in each
                ]
                norm_now = norm_next
        for i in each:
            solved[kind, i] = answer[i]

    b_done = {}

    def state_cols(place):
        return pl.ds(pl.multiple_of(place * SPAN, SPAN), SPAN)

    def read(kind):
        gain = pick_row(gain_ref[...], me)
        here = token_rows(kind)
        each = range(inner)
        bs = [block_of(kind, i) for i in each]
        answers = [solved[kind, i] for i in each]
        corr = [correlate(answers[i], bs[i]) for i in each]
        left = [
            jnp.concatenate(
                [
                    (carried[bs[i], here, :] * answers[i]).astype(BF16),
                    (corr[i] * weights[bs[i], here, :]).astype(BF16),
                ],
                axis=1,
            )
            for i in each
        ]
        mixed = [
            jnp.concatenate([start_state(1, b).astype(BF16), vb[block_rows(b), :]], axis=0)
            for b in bs
        ]
        raws = [jnp.dot(left[i], mixed[i], preferred_element_type=F32) for i in each]
        scales = [
            lax.rsqrt(jnp.mean(raw * raw, axis=-1, keepdims=True) + EPSILON) for raw in raws
        ]
        results_of = [(raws[i] * scales[i] * gain).astype(BF16) for i in each]
        for i in each:
            o = i + 1
            normed = results_of[i]
            if o == inner:
                readout[kind, :, state_cols(me)] = normed
            else:
                sending[kind, i] = normed
        for i in range(inner - 1):
            o = i + 1
            copy = remote(
                sending.at[kind, i], readout.at[kind, :, state_cols(me)],
                b_send.at[kind, o], b_recv.at[kind, o], plane[3](shift_plane(o, 1)),
            )
            copy.start()
            pending.append(copy.wait_send)
            back = shift_plane(o, -1)
            b_done[kind, o] = remote(
                sending.at[kind, i], readout.at[kind, :, state_cols(back)],
                b_send.at[kind, o], b_recv.at[kind, o], plane[3](back),
            ).wait_recv

    def wait_readout(kind):
        for o in range(1, inner):
            b_done.pop((kind, o))()

    tiles = half // TILE
    far, near_1, near_2, _ = chunks

    def tile_cols(side, c):
        return slice(side * half + c * TILE, side * half + (c + 1) * TILE)

    def project(kind, side, c):
        return jnp.dot(
            readout[kind], wv[:, tile_cols(side, c)], preferred_element_type=F32
        )

    def result_copy(i, c, kind, side, landing, peer):
        return remote(
            partial.at[kind, :, tile_cols(side, c)], landing.at[:, tile_cols(0, c)],
            r_send.at[i, c], r_recv.at[i, c], (s, peer),
        )

    results = [
        lambda c: result_copy(0, c, 0, 0, relay_a, near_1),
        lambda c: result_copy(1, c, 0, 1, relay_b, near_2),
        lambda c: result_copy(2, c, 1, 0, n1_a, near_1),
        lambda c: result_copy(3, c, 1, 1, n1_b, near_1),
        lambda c: result_copy(4, c, 2, 1, n2_b, near_2),
        lambda c: result_copy(5, c, 2, 0, n2_a, near_2),
    ]

    def send_tiles(cs, batch):
        for c in cs:
            values = [project(kind, side, c) for _, kind, side in batch]
            for (_, kind, side), value in zip(batch, values):
                partial[kind, :, tile_cols(side, c)] = value.astype(BF16)
        for c in cs:
            for i, _, _ in batch:
                results[i](c).start()

    for kind in range(3):
        if kind > 0:
            wait_queries(kind)
        solve(kind)
        read(kind)
    w_copy.wait()
    wait_readout(0)
    for c in range(0, tiles, 2):
        send_tiles((c, c + 1), ((0, 0, 0), (1, 0, 1)))
    wait_readout(1)
    send_tiles(range(tiles), ((2, 1, 0),))
    wait_readout(2)
    send_tiles(range(tiles), ((4, 2, 1),))
    wait_queries(3)
    solve(3)
    read(3)
    for c in range(tiles):
        here = tile_cols(0, c)
        values = project(1, 1, c), project(2, 0, c)
        own[:, here], own[:, tile_cols(1, c)] = values
    for c in range(tiles):
        results[1](c).wait_recv()
        results[0](c).wait_recv()
        here = tile_cols(0, c)
        there = tile_cols(1, c)
        partial[1, :, there] = (own[:, here] + relay_b[:, here].astype(F32)).astype(BF16)
        partial[2, :, here] = (own[:, there] + relay_a[:, here].astype(F32)).astype(BF16)
        results[3](c).start()
        results[5](c).start()
    wait_readout(3)
    for c in range(tiles):
        for side in range(2):
            own[:, tile_cols(side, c)] = project(3, side, c)

    for c in range(tiles):
        for side, (i1, from_1), (i2, from_2) in (
            (0, (2, n1_a), (5, n2_a)),
            (1, (3, n1_b), (4, n2_b)),
        ):
            results[i1](c).wait_recv()
            results[i2](c).wait_recv()
            cols = tile_cols(side, c)
            out_ref[:, cols] = (
                own[:, cols]
                + from_1[:, tile_cols(0, c)].astype(F32)
                + from_2[:, tile_cols(0, c)].astype(F32)
            ).astype(BF16)

    for result in results:
        for c in range(tiles):
            result(c).wait_send()
    for fn in pending:
        fn()


def body(planes, inner, query_rows, key_rows, value_rows, log_decay, regularizer, norm_gain, out_weight):
    ring = lax.axis_size("head")
    rows, model = query_rows.shape
    heads = regularizer.shape[0]
    tokens = rows * ring * inner
    blocks = tokens // SPAN
    half = model // 2
    piece = SPAN // planes
    vm = pltpu.VMEM
    dma = pltpu.SemaphoreType.DMA
    scratch = [
        vm((inner,) + log_decay.shape, F32),
        pltpu.SMEM(regularizer.shape, F32),
        vm(norm_gain.shape, F32),
        vm((tokens, SPAN), BF16),
        vm((tokens, SPAN), BF16),
        vm((tokens, SPAN), BF16),
        vm((heads * SPAN, model), BF16),
        vm((blocks, SPAN, SPAN), F32),
        vm((blocks, SPAN, SPAN), F32),
        vm((blocks, SPAN, SPAN), F32),
        vm((blocks, 8, SPAN), F32),
        vm((blocks, 8, SPAN), F32),
        vm((blocks, 8, SPAN), F32),
        vm((8, SPAN), F32),
        vm((blocks, 2 * SPAN, SPAN), BF16),
        vm((blocks, SPAN, SPAN), BF16),
        vm((blocks, SPAN, SPAN), F32),
        vm((2, blocks, SPAN, SPAN), F32),
        vm((planes, 4 * piece, SPAN), BF16),
        vm((planes, 4 * piece, SPAN), BF16),
        vm((planes, 3 * piece, SPAN), BF16),
        vm((planes, 3 * piece, SPAN), BF16),
        vm((2, SPAN, SPAN), F32),
        vm((ring, inner, rows, SPAN), F32),
        vm((ring, inner - 1, rows, SPAN), BF16),
        vm((ring, rows, heads * SPAN), BF16),
        vm((rows, model), F32),
        vm((ring - 1, rows, model), BF16),
    ]
    scratch += [vm((rows, half), BF16)] * 6
    scratch += [dma((7,))] + [dma((inner,))] * 2 + [dma((3, inner * ring))] * 2
    scratch += [dma((planes,))] * 4 + [dma((ring, inner))] * 2
    scratch += [dma((6, half // TILE))] * 2
    in_hbm = pl.BlockSpec(memory_space=pltpu.HBM)
    return pl.pallas_call(
        functools.partial(kernel, planes, inner, ring),
        out_shape=pltpu.VMEM((rows, model), BF16),
        in_specs=[in_hbm] * 7,
        out_specs=pl.BlockSpec(memory_space=pltpu.VMEM),
        scratch_shapes=scratch,
        compiler_params=pltpu.CompilerParams(
            collective_id=0, has_side_effects=True, vmem_limit_bytes=60 * 1024 * 1024
        ),
    )(query_rows, key_rows, value_rows, log_decay, regularizer, norm_gain, out_weight)


def solution(mesh):
    placed = (
        P(("seq", "head"), None),
        P(("seq", "head"), None),
        P(("seq", "head"), None),
        P("head", "seq"),
        P("head"),
        P("head", None),
        P("head", None),
    )
    inner = 8
    planes = mesh.shape["seq"] // inner
    return jax.shard_map(
        functools.partial(body, planes, inner), mesh=mesh, in_specs=placed,
        out_specs=P(("seq", "head"), None), check_vma=False,
    )
```

```python
import functools

import jax
import jax.numpy as jnp
from jax import lax
from jax.experimental import pallas as pl
from jax.experimental.pallas import tpu as pltpu
from jax.sharding import PartitionSpec as P

SPAN = 128
ITERS = 4
EPSILON = 1e-06
TILE = 512
BATCH = 1
MESH = pl.DeviceIdType.MESH
HIGHEST = lax.Precision.HIGHEST
F32 = jnp.float32
BF16 = jnp.bfloat16
ROWS_BY_ROWS = (((1,), (1,)), ((), ()))
COLS_BY_COLS = (((0,), (0,)), ((), ()))


def kernel(
    planes, inner, ring,
    q_hbm, k_hbm, v_hbm, ld_hbm, reg_hbm, gain_hbm, w_hbm, out_ref,
    ld_plane, reg_ref, gain_ref, qb, kb, vb, wv, weights, carried, tails, leave, enter, to_end, dec_total,
    kpair, tailed, terms, before, z_to, z_in, z_out, z_back, z_state,
    solved, sending, readout, own, partial,
    relay_a, relay_b, n1_a, n1_b, n2_a, n2_b,
    local_sem, ld_send, ld_recv, g_send, g_recv,
    z_send, z_recv, zb_send, zb_recv, b_send, b_recv, r_send, r_recv,
):
    s = lax.axis_index("seq")
    x = lax.axis_index("head")
    z = lax.div(s, inner)
    me = lax.rem(s, inner)
    rows = q_hbm.shape[0]
    blocks = kpair.shape[0]
    per_device = blocks // inner
    half = w_hbm.shape[1] // 2
    pending = []

    def loop(lo, hi, fn):
        def step(i, carry):
            fn(i)
            return carry
        lax.fori_loop(lo, hi, step, 0)

    def shift_plane(o, sign):
        return lax.rem(me + inner + sign * o, inner)

    def shift_z(o, sign):
        return lax.rem(z + planes + sign * o, planes)

    def shift_group(o, sign):
        over = lax.div(o, ring)
        along = lax.rem(o, ring)
        return (
            lax.rem(me + inner + sign * over, inner), lax.rem(x + ring + sign * along, ring)
        )

    def shift_far(mask):
        return lambda o, sign: (lax.rem(me + inner + sign * o, inner), x ^ mask)

    def in_group(peer):
        return (z * inner + peer[0], peer[1])

    plane = (1, inner, shift_plane, lambda peer: (z * inner + peer, x))
    column = (1, planes, shift_z, lambda peer: (peer * inner + me, x))
    group = (1, inner * ring, shift_group, in_group)
    kinds = [(0 if mask else 1, inner, shift_far(mask), in_group) for mask in (2, 3, 1, 0)]

    def remote(src, dst, send, recv, device):
        return pltpu.make_async_remote_copy(
            src_ref=src, dst_ref=dst, send_sem=send, recv_sem=recv,
            device_id=device, device_id_type=MESH,
        )

    def exchange(partners, make_pair, send, recv, here, later=False):
        first, count, shift, device = partners

        def copy(o, sign):
            peer = shift(o, sign)
            src, dst = make_pair(peer, here) if sign == 1 else make_pair(here, peer)
            return remote(src, dst, send(o), recv(o), device(peer))

        pending.append(lambda: loop(first, count, lambda o: copy(o, 1).wait_send()))
        if later:
            return (lambda o: copy(o, 1).start()), (lambda o: copy(o, -1).wait_recv())
        for o in range(first, count):
            copy(o, 1).start()
        return lambda o: copy(o, -1).wait_recv()

    def all_of(partners, got):
        loop(partners[0], partners[1], got)

    small = [
        pltpu.make_async_copy(src, dst, local_sem.at[i])
        for i, (src, dst) in enumerate(
            ((ld_hbm, ld_plane.at[me]), (reg_hbm, reg_ref), (gain_hbm, gain_ref))
        )
    ]
    for copy in small:
        copy.start()

    barrier = pltpu.get_barrier_semaphore()
    for _, count, shift, device in (group, column):
        loop(
            1, count,
            lambda o, shift=shift, device=device: pl.semaphore_signal(
                barrier, inc=1, device_id=device(shift(o, 1)), device_id_type=MESH
            ),
        )
    pl.semaphore_wait(barrier, inner * ring - 1 + planes - 1)

    got_ld = exchange(
        plane, lambda to, frm: (ld_hbm, ld_plane.at[frm]),
        lambda o: ld_send.at[o], lambda o: ld_recv.at[o], me,
    )

    def slot(place):
        return pl.ds(pl.multiple_of((place[0] * ring + place[1]) * rows, rows), rows)

    def head_cols(place):
        return pl.ds(pl.multiple_of((place[1] * inner + place[0]) * SPAN, SPAN), SPAN)

    got_group = []
    for i, (src_hbm, dst_buf) in enumerate(((k_hbm, kb), (v_hbm, vb), (q_hbm, qb))):
        def make(to, frm, src_hbm=src_hbm, dst_buf=dst_buf):
            return src_hbm.at[:, head_cols(to)], dst_buf.at[slot(frm), :]

        mine = pltpu.make_async_copy(*make((me, x), (me, x)), local_sem.at[3 + i])
        mine.start()
        parts = [group] if i < 2 else kinds
        moves = [
            exchange(
                part, make,
                lambda o, i=i, at=n * inner: g_send.at[i, at + o],
                lambda o, i=i, at=n * inner: g_recv.at[i, at + o],
                (me, x), later=True,
            )
            for n, part in enumerate(parts)
        ]
        got_group.append((mine, moves))

    def go_group(i, n=0):
        part = group if i < 2 else kinds[n]
        loop(part[0], part[1], got_group[i][1][n][0])

    go_group(0)
    go_group(1)
    w_copy = pltpu.make_async_copy(w_hbm, wv, local_sem.at[6])

    def pick_row(table, i):
        place = lax.broadcasted_iota(jnp.int32, table.shape, 0)
        return jnp.sum(jnp.where(place == i, table, 0.0), axis=0, keepdims=True)

    row_id = lax.broadcasted_iota(jnp.int32, (SPAN, SPAN), 0)
    col_id = lax.broadcasted_iota(jnp.int32, (SPAN, SPAN), 1)
    causal = row_id >= col_id
    for copy in small:
        copy.wait()
    all_of(plane, got_ld)

    def down(row):
        return jnp.transpose(jnp.broadcast_to(row, (SPAN, SPAN)))

    sums = lax.dot_general(
        jnp.concatenate(
            [
                pick_row(ld_plane[b // per_device][:, (b % per_device) * SPAN:(b % per_device + 1) * SPAN], me)
                for b in range(blocks)
            ],
            axis=0,
        ),
        jnp.where(causal, 1.0, 0.0).astype(F32),
        ROWS_BY_ROWS, precision=HIGHEST, preferred_element_type=F32,
    )
    total = jnp.zeros((8, SPAN), F32)
    for b in range(blocks):
        row = sums[b:b + 1, :]
        last = jnp.broadcast_to(row[:, SPAN - 1:SPAN], (8, SPAN))
        enter[b] = jnp.exp(total)
        total = total + last
        to_end[b] = total
        cum = down(row)
        tails[b] = jnp.exp(last[0:1, :] - cum)
        weights[b] = jnp.where(causal, jnp.exp(jnp.minimum(cum - row, 0.0)), 0.0)
        carried[b] = jnp.exp(cum)
        leave[b] = jnp.exp(last)
    dec_total[...] = total
    for b in range(blocks):
        to_end[b] = jnp.exp(total - to_end[b])

    def split(value):
        high = value.astype(BF16)
        return high, (value - high.astype(F32)).astype(BF16)

    def block_rows(b):
        return pl.ds(pl.multiple_of(b * SPAN, SPAN), SPAN)

    def plane_states(t):
        mine, ((_, got),) = got_group[t]

        def states(overs, acc):
            bs = [
                lax.rem(me + inner - over, inner) * per_device + n
                for over in overs
                for n in range(per_device)
            ]
            if t == 0:
                keys = [kb[block_rows(b), :].astype(F32) for b in bs]
                scales = [
                    lax.rsqrt(jnp.mean(key * key, axis=-1, keepdims=True) + EPSILON)
                    * SPAN ** -0.5
                    for key in keys
                ]
                normed = [key * scale for key, scale in zip(keys, scales)]
                pairs = [split(value) for value in normed]
                lefts = [split(tails[b] * value) for b, value in zip(bs, normed)]
                products = [
                    lax.dot_general(
                        jnp.concatenate([left[0], left[1], left[0]], axis=0),
                        jnp.concatenate([pair[0], pair[0], pair[1]], axis=0),
                        COLS_BY_COLS, preferred_element_type=F32,
                    )
                    for left, pair in zip(lefts, pairs)
                ]
                for b, pair, left in zip(bs, pairs, lefts):
                    kpair[b, :SPAN, :], kpair[b, SPAN:, :] = pair
                    tailed[b] = left[0]
            else:
                products = [
                    lax.dot_general(
                        tailed[b], vb[block_rows(b), :], COLS_BY_COLS,
                        preferred_element_type=F32,
                    )
                    for b in bs
                ]
            for b, product in zip(bs, products):
                terms[b] = product
                acc = acc + to_end[b][0:1, :] * product
            return acc

        mine.wait()
        loop(1, BATCH * ring, got)
        plane_total = states(list(range(BATCH)), jnp.zeros((SPAN, SPAN), F32))

        def batch(i, acc):
            loop(i * BATCH * ring, (i + 1) * BATCH * ring, got)
            return states([i * BATCH + n for n in range(BATCH)], acc)

        plane_total = lax.fori_loop(1, inner // BATCH, batch, plane_total)
        for i in range(planes):
            rows_of = plane_total[i * piece:(i + 1) * piece, :]
            if t == 0:
                z_to[i, 0:piece, :], z_to[i, piece:2 * piece, :] = split(rows_of)
            else:
                z_to[i, 2 * piece:3 * piece, :] = rows_of.astype(BF16)

    def block_starts(t):
        acc = jnp.zeros((SPAN, SPAN), F32)
        for b in range(0, blocks, 2):
            factors = leave[b][0:1, :], leave[b + 1][0:1, :]
            added = terms[b], terms[b + 1]
            middle = factors[0] * acc + added[0]
            before[t, b], before[t, b + 1] = acc, middle
            acc = factors[1] * middle + added[1]

    piece = SPAN // planes

    def pack_decay():
        rest = dec_total[0:1, :]
        terms_of = []
        for _ in range(3):
            term = rest.astype(BF16)
            terms_of.append(jnp.broadcast_to(term.astype(F32), (8, SPAN)))
            rest = rest - term.astype(F32)
        place = lax.broadcasted_iota(jnp.int32, (piece, SPAN), 0)
        packed = jnp.zeros((piece, SPAN), F32)
        for i, term in enumerate(terms_of):
            packed = jnp.where(place == i, term[0:1, :], packed)
        packed = packed.astype(BF16)
        for i in range(planes):
            z_to[i, 3 * piece:4 * piece, :] = packed

    def send_z():
        got = exchange(
            column, lambda to, frm: (z_to.at[to], z_in.at[frm]),
            lambda o: z_send.at[o], lambda o: z_recv.at[o], z,
        )
        z_in[z] = z_to[z]
        return got

    def z_prefix():
        arrived = [z_in[i].astype(F32) for i in range(planes - 1)]
        tails_in = [part[3 * piece:4 * piece, :] for part in arrived]
        decays = [jnp.exp(tail[0:1, :] + tail[1:2, :] + tail[2:3, :]) for tail in tails_in]
        grams = [jnp.zeros((piece, SPAN), F32)]
        memories = [grams[0]]
        for part, decay in zip(arrived, decays):
            grams.append(decay * grams[-1] + (part[0:piece, :] + part[piece:2 * piece, :]))
            memories.append(decay * memories[-1] + part[2 * piece:3 * piece, :])
        for i in range(planes):
            z_out[i, 0:piece, :], z_out[i, piece:2 * piece, :] = split(grams[i])
            z_out[i, 2 * piece:3 * piece, :] = memories[i].astype(BF16)

    def send_z_back():
        got = exchange(
            column, lambda to, frm: (z_out.at[to], z_back.at[frm]),
            lambda o: zb_send.at[o], lambda o: zb_recv.at[o], z,
        )
        z_back[z] = z_out[z]
        return got

    def collect():
        arrived = [z_back[i].astype(F32) for i in range(planes)]
        for i in range(planes):
            here = slice(i * piece, (i + 1) * piece)
            z_state[0, here, :] = arrived[i][0:piece, :] + arrived[i][piece:2 * piece, :]
            z_state[1, here, :] = arrived[i][2 * piece:3 * piece, :]

    def wait_queries(kind):
        mine, moves = got_group[2]
        if kind == 3:
            mine.wait()
        all_of(kinds[kind], moves[kind][1])

    pack_decay()
    plane_states(0)
    block_starts(0)
    plane_states(1)
    got_z = send_z()
    go_group(2, 0)
    go_group(2, 1)
    block_starts(1)
    all_of(column, got_z)
    z_prefix()
    got_zb = send_z_back()
    go_group(2, 2)
    go_group(2, 3)
    w_copy.start()
    wait_queries(0)
    all_of(column, got_zb)
    collect()

    def start_state(t, b):
        return enter[b][0:1, :] * z_state[t] + before[t, b]

    def row_sum(a):
        return jnp.sum(a, axis=-1, keepdims=True)

    chunks = [x ^ mask for mask in (2, 3, 1, 0)]

    def member(i):
        return lax.rem(me + 1 + i, inner)

    def block_of(kind, i):
        return member(i) * per_device + lax.div(chunks[kind], ring // per_device)

    def token_rows(kind):
        return pl.ds(
            pl.multiple_of(lax.rem(chunks[kind], ring // per_device) * rows, rows), rows
        )

    def correlate(vector, b):
        return add_terms(
            lax.dot_general(
                jnp.concatenate(split(vector), axis=0), kpair[b], ROWS_BY_ROWS,
                preferred_element_type=F32,
            )
        )

    def add_terms(products):
        high, low = products[:rows, :], products[rows:, :]
        return high[:, :SPAN] + (high[:, SPAN:] + low[:, :SPAN])

    def solve(kind):
        each = range(inner)
        bs = [block_of(kind, i) for i in each]
        here = token_rows(kind)
        ridge = reg_ref[me]
        states = [split(start_state(0, b)) for b in bs]
        mixed = [
            jnp.concatenate(
                [
                    jnp.concatenate(states[i], axis=1),
                    jnp.concatenate([kpair[bs[i], :SPAN, :], kpair[bs[i], SPAN:, :]], axis=1),
                ],
                axis=0,
            )
            for i in each
        ]
        direction = [qb[slot((member(i), chunks[kind])), :].astype(F32) for i in each]
        residual = list(direction)
        answer = [None] * inner
        norm_now = [row_sum(r * r) for r in residual]
        for turn in range(ITERS):
            corr = [correlate(direction[i], bs[i]) for i in each]
            from_state = [split(carried[bs[i], here, :] * direction[i]) for i in each]
            from_block = [split(corr[i] * weights[bs[i], here, :]) for i in each]
            both = [
                jnp.concatenate(
                    [
                        jnp.concatenate([from_state[i][n], from_block[i][n]], axis=1)
                        for n in range(2)
                    ],
                    axis=0,
                )
                for i in each
            ]
            mapped = [
                add_terms(jnp.dot(both[i], mixed[i], preferred_element_type=F32))
                + ridge * direction[i]
                for i in each
            ]
            step_size = [norm_now[i] / row_sum(direction[i] * mapped[i]) for i in each]
            answer = [
                step_size[i] * direction[i]
                if turn == 0
                else answer[i] + step_size[i] * direction[i]
                for i in each
            ]
            if turn + 1 < ITERS:
                residual = [residual[i] - step_size[i] * mapped[i] for i in each]
                norm_next = [row_sum(r * r) for r in residual]
                direction = [
                    residual[i] + norm_next[i] / norm_now[i] * direction[i] for i in each
                ]
                norm_now = norm_next
        for i in each:
            solved[kind, i] = answer[i]

    b_done = {}

    def state_cols(place):
        return pl.ds(pl.multiple_of(place * SPAN, SPAN), SPAN)

    def read(kind):
        gain = pick_row(gain_ref[...], me)
        here = token_rows(kind)
        each = range(inner)
        bs = [block_of(kind, i) for i in each]
        answers = [solved[kind, i] for i in each]
        corr = [correlate(answers[i], bs[i]) for i in each]
        left = [
            jnp.concatenate(
                [
                    (carried[bs[i], here, :] * answers[i]).astype(BF16),
                    (corr[i] * weights[bs[i], here, :]).astype(BF16),
                ],
                axis=1,
            )
            for i in each
        ]
        mixed = [
            jnp.concatenate([start_state(1, b).astype(BF16), vb[block_rows(b), :]], axis=0)
            for b in bs
        ]
        raws = [jnp.dot(left[i], mixed[i], preferred_element_type=F32) for i in each]
        scales = [
            lax.rsqrt(jnp.mean(raw * raw, axis=-1, keepdims=True) + EPSILON) for raw in raws
        ]
        results_of = [(raws[i] * scales[i] * gain).astype(BF16) for i in each]
        for i in each:
            o = i + 1
            normed = results_of[i]
            if o == inner:
                readout[kind, :, state_cols(me)] = normed
            else:
                sending[kind, i] = normed
        for i in range(inner - 1):
            o = i + 1
            copy = remote(
                sending.at[kind, i], readout.at[kind, :, state_cols(me)],
                b_send.at[kind, o], b_recv.at[kind, o], plane[3](shift_plane(o, 1)),
            )
            copy.start()
            pending.append(copy.wait_send)
            back = shift_plane(o, -1)
            b_done[kind, o] = remote(
                sending.at[kind, i], readout.at[kind, :, state_cols(back)],
                b_send.at[kind, o], b_recv.at[kind, o], plane[3](back),
            ).wait_recv

    def wait_readout(kind):
        for o in range(1, inner):
            b_done.pop((kind, o))()

    tiles = half // TILE
    far, near_1, near_2, _ = chunks

    def tile_cols(side, c):
        return slice(side * half + c * TILE, side * half + (c + 1) * TILE)

    def project(kind, side, c):
        return jnp.dot(
            readout[kind], wv[:, tile_cols(side, c)], preferred_element_type=F32
        )

    def result_copy(i, c, kind, side, landing, peer):
        return remote(
            partial.at[kind, :, tile_cols(side, c)], landing.at[:, tile_cols(0, c)],
            r_send.at[i, c], r_recv.at[i, c], (s, peer),
        )

    results = [
        lambda c: result_copy(0, c, 0, 0, relay_a, near_1),
        lambda c: result_copy(1, c, 0, 1, relay_b, near_2),
        lambda c: result_copy(2, c, 1, 0, n1_a, near_1),
        lambda c: result_copy(3, c, 1, 1, n1_b, near_1),
        lambda c: result_copy(4, c, 2, 1, n2_b, near_2),
        lambda c: result_copy(5, c, 2, 0, n2_a, near_2),
    ]

    def send_tiles(cs, batch):
        for c in cs:
            values = [project(kind, side, c) for _, kind, side in batch]
            for (_, kind, side), value in zip(batch, values):
                partial[kind, :, tile_cols(side, c)] = value.astype(BF16)
        for c in cs:
            for i, _, _ in batch:
                results[i](c).start()

    for kind in range(3):
        if kind > 0:
            wait_queries(kind)
        solve(kind)
        read(kind)
    w_copy.wait()
    wait_readout(0)
    for c in range(0, tiles, 2):
        send_tiles((c, c + 1), ((0, 0, 0), (1, 0, 1)))
    wait_readout(1)
    send_tiles(range(tiles), ((2, 1, 0),))
    wait_readout(2)
    send_tiles(range(tiles), ((4, 2, 1),))
    wait_queries(3)
    solve(3)
    read(3)
    for c in range(tiles):
        here = tile_cols(0, c)
        values = project(1, 1, c), project(2, 0, c)
        own[:, here], own[:, tile_cols(1, c)] = values
    for c in range(tiles):
        results[1](c).wait_recv()
        results[0](c).wait_recv()
        here = tile_cols(0, c)
        there = tile_cols(1, c)
        partial[1, :, there] = (own[:, here] + relay_b[:, here].astype(F32)).astype(BF16)
        partial[2, :, here] = (own[:, there] + relay_a[:, here].astype(F32)).astype(BF16)
        results[3](c).start()
        results[5](c).start()
    wait_readout(3)
    for c in range(tiles):
        for side in range(2):
            own[:, tile_cols(side, c)] = project(3, side, c)

    for c in range(tiles):
        for side, (i1, from_1), (i2, from_2) in (
            (0, (2, n1_a), (5, n2_a)),
            (1, (3, n1_b), (4, n2_b)),
        ):
            results[i1](c).wait_recv()
            results[i2](c).wait_recv()
            cols = tile_cols(side, c)
            out_ref[:, cols] = (
                own[:, cols]
                + from_1[:, tile_cols(0, c)].astype(F32)
                + from_2[:, tile_cols(0, c)].astype(F32)
            ).astype(BF16)

    for result in results:
        for c in range(tiles):
            result(c).wait_send()
    for fn in pending:
        fn()


def body(planes, inner, query_rows, key_rows, value_rows, log_decay, regularizer, norm_gain, out_weight):
    ring = lax.axis_size("head")
    rows, model = query_rows.shape
    heads = regularizer.shape[0]
    tokens = rows * ring * inner
    blocks = tokens // SPAN
    half = model // 2
    piece = SPAN // planes
    vm = pltpu.VMEM
    dma = pltpu.SemaphoreType.DMA
    scratch = [
        vm((inner,) + log_decay.shape, F32),
        pltpu.SMEM(regularizer.shape, F32),
        vm(norm_gain.shape, F32),
        vm((tokens, SPAN), BF16),
        vm((tokens, SPAN), BF16),
        vm((tokens, SPAN), BF16),
        vm((heads * SPAN, model), BF16),
        vm((blocks, SPAN, SPAN), F32),
        vm((blocks, SPAN, SPAN), F32),
        vm((blocks, SPAN, SPAN), F32),
        vm((blocks, 8, SPAN), F32),
        vm((blocks, 8, SPAN), F32),
        vm((blocks, 8, SPAN), F32),
        vm((8, SPAN), F32),
        vm((blocks, 2 * SPAN, SPAN), BF16),
        vm((blocks, SPAN, SPAN), BF16),
        vm((blocks, SPAN, SPAN), F32),
        vm((2, blocks, SPAN, SPAN), F32),
        vm((planes, 4 * piece, SPAN), BF16),
        vm((planes, 4 * piece, SPAN), BF16),
        vm((planes, 3 * piece, SPAN), BF16),
        vm((planes, 3 * piece, SPAN), BF16),
        vm((2, SPAN, SPAN), F32),
        vm((ring, inner, rows, SPAN), F32),
        vm((ring, inner - 1, rows, SPAN), BF16),
        vm((ring, rows, heads * SPAN), BF16),
        vm((rows, model), F32),
        vm((ring - 1, rows, model), BF16),
    ]
    scratch += [vm((rows, half), BF16)] * 6
    scratch += [dma((7,))] + [dma((inner,))] * 2 + [dma((3, inner * ring))] * 2
    scratch += [dma((planes,))] * 4 + [dma((ring, inner))] * 2
    scratch += [dma((6, half // TILE))] * 2
    in_hbm = pl.BlockSpec(memory_space=pltpu.HBM)
    return pl.pallas_call(
        functools.partial(kernel, planes, inner, ring),
        out_shape=pltpu.VMEM((rows, model), BF16),
        in_specs=[in_hbm] * 7,
        out_specs=pl.BlockSpec(memory_space=pltpu.VMEM),
        scratch_shapes=scratch,
        compiler_params=pltpu.CompilerParams(
            collective_id=0, has_side_effects=True, vmem_limit_bytes=60 * 1024 * 1024
        ),
    )(query_rows, key_rows, value_rows, log_decay, regularizer, norm_gain, out_weight)


def solution(mesh):
    placed = (
        P(("seq", "head"), None),
        P(("seq", "head"), None),
        P(("seq", "head"), None),
        P("head", "seq"),
        P("head"),
        P("head", None),
        P("head", None),
    )
    inner = 8
    planes = mesh.shape["seq"] // inner
    return jax.shard_map(
        functools.partial(body, planes, inner), mesh=mesh, in_specs=placed,
        out_specs=P(("seq", "head"), None), check_vma=False,
    )
```
